32 devices in a mesh: rx: 4 (over x, core), ry: 4 (over z), tp: 2 (over y).
Axes of the slice: x: 2, y: 2, z: 4, core: 2. Of those that a mesh axis runs over, the one named last changes fastest.
Arguments:
- weights: float32 [4, 4, 2, 8192, 1024], P('rx', 'ry', None, 'tp'), may hold values from -6 to 6
- factors_rx: float32 [4, 4, 2, 8, 1024], P('rx', 'ry'), may hold values from -6 to 6
- factors_ry: float32 [4, 4, 2, 8, 1024], P('rx', 'ry'), may hold values from -6 to 6
Outputs:
- mixed_weights: float32 [4, 4, 2, 8192, 1024], P('rx', 'ry', None, 'tp')
- next_rx: float32 [4, 4, 2, 8, 1024], P('rx', 'ry')
- next_ry: float32 [4, 4, 2, 8, 1024], P('rx', 'ry')
The draws below stay inside these ranges and needn't reach their ends.
All inputs are finite; a program needn't handle non-finite values.
Results may differ from the reference program's by a relative error of at most 0.00007.
Values sent between devices are 32-bit elements; how exact they have to be, the bound alone decides.
No kernel may reach another device: no remote copies, remote signals or barrier semaphores. Data moves between devices by JAX's collectives and lax.ppermute only.
A program may use at most 128 MiB of HBM per device.

```python
import jax
import jax.numpy as jnp
from jax import lax

D = 8192
KV = 1024
RANK = 8
MATS = 2
REP_X = 4
REP_Y = 4


def steps_of(own_key, shape, cuts, low, top_value):
    def one(position, parts):
        steps = jax.random.uniform(jax.random.fold_in(jax.random.fold_in(own_key, 6), position), (parts,), jnp.float32, low / len(cuts), top_value / len(cuts))
        return jnp.repeat(jnp.exp(steps), shape[position] // parts).reshape((-1,) + (1,) * (len(shape) - position - 1))

    loudness = one(*cuts[0])
    for cut in cuts[1:]:
        loudness = loudness * one(*cut)
    return loudness


def noise(rng, dims, scale, most, split=(), kind=jnp.bfloat16):
    array = jax.random.normal(rng, dims, jnp.float32) * scale
    if len(split) > 0:
        array = steps_of(rng, dims, split, -0.22, 0.18) * array
    return jnp.clip(array, min=-most, max=most).astype(kind)


def setup_inputs(seed: int = 0) -> dict:
    arg_keys = jax.random.split(jax.random.key(seed), 4)
    weights = noise(arg_keys[0], (REP_X, REP_Y, MATS, D, KV), 1.0, 6.0, ((0, 4), (1, 4), (3, 2)), jnp.float32)
    factors_rx = noise(arg_keys[1], (REP_X, REP_Y, MATS, RANK, KV), 1.0, 6.0, ((0, 4), (1, 4)), jnp.float32)
    factors_ry = noise(arg_keys[2], (REP_X, REP_Y, MATS, RANK, KV), 1.0, 6.0, ((0, 4), (1, 4)), jnp.float32)
    return dict(weights=weights, factors_rx=factors_rx, factors_ry=factors_ry)


highest = lax.Precision.HIGHEST
mixing = 0.2

def across(values):
    return jnp.stack([jnp.roll(values[:, :, 1], -1, 0), jnp.roll(values[:, :, 0], 1, 0), jnp.roll(values[:, :, 3], -1, 1), jnp.roll(values[:, :, 2], 1, 1)], 2)

def reference(weights, factors_rx, factors_ry):
    factor_set = jnp.stack([factors_rx, jnp.roll(factors_rx, 1, 0), factors_ry, jnp.roll(factors_ry, 1, 1)], 2)
    projected = jnp.einsum('abemrk,abmdk->abemrd', factor_set, weights, precision=highest)
    differ = projected - across(projected)
    gram_sums = jnp.einsum('abemrd,abemsd->abemrs', differ, differ, precision=highest)
    lower_factor = jnp.linalg.cholesky(gram_sums)
    normalised = lax.linalg.triangular_solve(lower_factor, differ, left_side=True, lower=True)
    back_terms = jnp.einsum('abemrd,abmdk->abemrk', normalised, weights, precision=highest)
    updated = back_terms + across(back_terms)
    correction = jnp.einsum('abemrd,abemrk->abmdk', normalised, updated, precision=highest)
    mixed_weights = weights - mixing * correction
    return (mixed_weights, updated[:, :, 0], updated[:, :, 2])
```

```python
import functools

import jax
import jax.numpy as jnp
from jax import lax
from jax.experimental import pallas as pl
from jax.experimental.pallas import tpu as pltpu
from jax.sharding import PartitionSpec as P

f32 = jnp.float32
bf16 = jnp.bfloat16
mixing = 0.2
edges = 4
mib = 1 << 20

NN = (((1,), (0,)), ((), ()))
NT = (((1,), (1,)), ((), ()))
TN = (((0,), (0,)), ((), ()))

in_vmem = pl.BlockSpec(memory_space=pltpu.VMEM)
in_hbm = pl.BlockSpec(memory_space=pltpu.HBM)


def vmem(value):
    return pltpu.with_memory_space_constraint(value, pltpu.VMEM)


def hbm(value):
    return pltpu.with_memory_space_constraint(value, pltpu.HBM)


def dot(a, b, dims):
    return lax.dot_general(a, b, dims, preferred_element_type=f32)


def split(value):
    high = value.astype(bf16)
    return high, (value - high.astype(f32)).astype(bf16)


def chunk_of(rows, most):
    size = min(rows, most)
    while rows % size:
        size //= 2
    return size


def shifted(value, axis, steps):
    count = lax.axis_size(axis)
    pairs = [(source, (source + steps) % count) for source in range(count)]
    return lax.ppermute(value, axis, pairs)


def from_partner(value, axis, distance):
    count = lax.axis_size(axis)
    return lax.ppermute(value, axis, [(i, i ^ distance) for i in range(count)])


def load_kernel(weights, held, sems):
    rows = held.shape[1]
    parts = sems.shape[0]
    size = rows // parts
    copies = [
        pltpu.make_async_copy(
            weights.at[0, 0, 0, pl.ds(i * size, size)], held.at[0, pl.ds(i * size, size)], sems.at[i]
        )
        for i in range(parts)
    ]
    for copy in copies:
        copy.start()
    for copy in copies:
        copy.wait()


def load(weights):
    return pl.pallas_call(
        load_kernel,
        name="load",
        out_shape=jax.ShapeDtypeStruct(weights.shape[2:], f32),
        in_specs=[in_hbm],
        out_specs=in_vmem,
        scratch_shapes=[pltpu.SemaphoreType.DMA((4,))],
        compiler_params=pltpu.CompilerParams(vmem_limit_bytes=4 * mib),
    )(hbm(weights))


def project_kernel(mat, chunk, following, same, f0, f1, f2, f3, *rest):
    if following:
        weights, o0, o1, o2, o3, held, sem = rest
        copy = pltpu.make_async_copy(weights.at[0, 0, mat + 1], held.at[mat + 1], sem)
        copy.start()
    else:
        o0, o1, o2, o3, held = rest
    rank = f0.shape[-2]
    high, low = split(jnp.concatenate([f[0, 0, mat] for f in (f0, f1, f2, f3)], 0))
    stack = jnp.concatenate(
        [jnp.concatenate([high, high], 1), jnp.concatenate([low, low], 1)], 0
    )
    width = edges * rank

    @pl.loop(0, held.shape[1] // chunk)
    def _(step):
        here = pl.ds(pl.multiple_of(step * chunk, chunk), chunk)
        w_high, w_low = split(held[mat, here, :])
        both = dot(stack, jnp.concatenate([w_high, w_low], 1), NT)
        total = both[:width] + both[width:]
        for edge, out in enumerate((o0, o1, o2, o3)):
            out[:, here] = total[edge * rank : (edge + 1) * rank]

    if following:
        copy.wait()


def project(held, factors, mat, weights=None):
    rows = held.shape[1]
    rank = factors[0].shape[-2]
    following = weights is not None
    shapes = [jax.ShapeDtypeStruct((rank, rows), f32)] * edges
    shapes = shapes + [jax.ShapeDtypeStruct(held.shape, f32)]
    scratch = []
    args = [vmem(held), *factors]
    in_specs = [in_vmem] * 5
    if following:
        args.append(hbm(weights))
        in_specs.append(in_hbm)
        scratch = [pltpu.SemaphoreType.DMA]
    return pl.pallas_call(
        functools.partial(project_kernel, mat, chunk_of(rows, 1024), following),
        name=f"project{mat}",
        out_shape=shapes,
        in_specs=in_specs,
        out_specs=[in_vmem] * (edges + 1),
        scratch_shapes=scratch,
        input_output_aliases={0: edges},
        compiler_params=pltpu.CompilerParams(vmem_limit_bytes=4 * mib),
    )(*args)


def back_kernel(mat, chunk, same, o0, o1, o2, o3, n0, n1, n2, n3, differ, sums, held):
    rank = o0.shape[0]
    width = edges * rank
    features = held.shape[2]
    sums[...] = jnp.zeros_like(sums)

    def body(step, gram):
        here = pl.ds(pl.multiple_of(step * chunk, chunk), chunk)
        p = jnp.concatenate(
            [o[:, here] - n[:, here] for o, n in zip((o0, o1, o2, o3), (n0, n1, n2, n3))], 0
        )
        differ[:, here] = p
        high, low = split(p)
        w_high, w_low = split(held[mat, here, :])
        pair = jnp.concatenate([high, low], 0)
        stack = jnp.concatenate([pair, pair], 1)
        both = dot(stack, jnp.concatenate([w_high, w_low], 0), NN)
        sums[:, :features] += both[:width] + both[width:]
        return gram + dot(pair, pair, NT)

    gram = lax.fori_loop(
        0, held.shape[1] // chunk, body, jnp.zeros((2 * width, 2 * width), f32)
    )
    total = (gram[:width, :width] + gram[width:, width:]) + (
        gram[:width, width:] + gram[width:, :width]
    )
    for edge in range(edges):
        here = slice(edge * rank, (edge + 1) * rank)
        sums[here, features : features + rank] = total[here, here]


def back(held, own, near, mat):
    _, rows, features = held.shape
    rank = own[0].shape[0]
    return pl.pallas_call(
        functools.partial(back_kernel, mat, chunk_of(rows, 1024)),
        name=f"back{mat}",
        out_shape=[
            jax.ShapeDtypeStruct((edges * rank, rows), f32),
            jax.ShapeDtypeStruct((edges * rank, features + 128), f32),
            jax.ShapeDtypeStruct(held.shape, f32),
        ],
        in_specs=[in_vmem] * 9,
        out_specs=[in_vmem] * 3,
        input_output_aliases={0: 2},
        compiler_params=pltpu.CompilerParams(vmem_limit_bytes=4 * mib),
    )(vmem(held), *own, *near)


def add_kernel(same, mine, other, b0, b1, b2, b3, gram, held):
    rank, features = b0.shape
    for edge, out in enumerate((b0, b1, b2, b3)):
        here = slice(edge * rank, (edge + 1) * rank)
        out[...] = mine[here, :features] + other[here, :features]
    gram[...] = mine[:, features:] + other[:, features:]


def add(held, mine, other, rank, mat):
    width, wide = mine.shape
    features = wide - 128
    return pl.pallas_call(
        add_kernel,
        name=f"add{mat}",
        out_shape=[jax.ShapeDtypeStruct((rank, features), f32)] * edges
        + [jax.ShapeDtypeStruct((width, 128), f32), jax.ShapeDtypeStruct(held.shape, f32)],
        in_specs=[in_vmem] * 3,
        out_specs=[in_vmem] * 6,
        input_output_aliases={0: 5},
        compiler_params=pltpu.CompilerParams(vmem_limit_bytes=4 * mib),
    )(vmem(held), mine, other)


def inverse_kernel(rank, same, gram, inverse, held):
    width = gram.shape[0]
    shape = (edges, rank, 128)
    row = lax.broadcasted_iota(jnp.int32, shape, 1)
    lane = lax.broadcasted_iota(jnp.int32, shape, 2)
    edge = lax.broadcasted_iota(jnp.int32, shape, 0)
    value = gram[...].reshape(shape)
    value = jnp.where(lane < rank, value, (lane == width + edge * rank + row).astype(f32))
    pivots = jnp.ones((edges, rank, 1), f32)
    for j in range(rank):
        pivot = value[:, j : j + 1, j : j + 1]
        pivots = jnp.where(row[:, :, :1] == j, pivot, pivots)
        factor = jnp.where(row > j, value[:, :, j : j + 1] / pivot, 0.0)
        value = value - factor * value[:, j : j + 1, :]
    value = value / jnp.sqrt(pivots)
    inverse[...] = value.reshape(width, 128)


def inverse_factor(held, gram, rank, mat):
    return pl.pallas_call(
        functools.partial(inverse_kernel, rank),
        name=f"inverse{mat}",
        out_shape=[
            jax.ShapeDtypeStruct(gram.shape, f32),
            jax.ShapeDtypeStruct(held.shape, f32),
        ],
        in_specs=[in_vmem] * 2,
        out_specs=[in_vmem] * 2,
        input_output_aliases={0: 1},
        compiler_params=pltpu.CompilerParams(vmem_limit_bytes=4 * mib),
    )(vmem(held), gram)


def mix_kernel(
    mat, chunk, slots, same, differ, inverse, b0, b1, b2, b3, n0, n1, n2, n3, *rest
):
    mixed, next_rx, next_ry, held, buffer, sems = rest[-6:]
    rank = b0.shape[0]
    width = edges * rank
    factor = inverse[:, width : 2 * width]
    sums = jnp.concatenate(
        [b[...] + n[...] for b, n in zip((b0, b1, b2, b3), (n0, n1, n2, n3))], 0
    )
    updated = lax.dot_general(
        factor, sums, NN, precision=lax.Precision.HIGHEST, preferred_element_type=f32
    )
    next_rx[...] = updated[:rank]
    next_ry[...] = updated[2 * rank : 3 * rank]
    right = mixing * lax.dot_general(
        factor, updated, TN, precision=lax.Precision.HIGHEST, preferred_element_type=f32
    )
    r_high, r_low = split(right)
    terms = jnp.concatenate([r_high, r_high, r_low, r_low], 0)
    steps = held.shape[1] // chunk

    def copy(step):
        slot = lax.rem(step, slots)
        return pltpu.make_async_copy(
            buffer.at[slot],
            mixed.at[0, 0, mat, pl.ds(pl.multiple_of(step * chunk, chunk), chunk)],
            sems.at[slot],
        )

    @pl.loop(0, steps)
    def _(step):
        here = pl.ds(pl.multiple_of(step * chunk, chunk), chunk)

        @pl.when(step >= slots)
        def _():
            copy(step - slots).wait()

        high, low = split(differ[:, here])
        lhs = jnp.concatenate([high, low, high, low], 0)
        buffer[lax.rem(step, slots)] = held[mat, here, :] - dot(lhs, terms, TN)
        copy(step).start()

    for step in range(max(steps - slots, 0), steps):
        copy(step).wait()


def mix(held, differ, inverse, sums, near, mat, shape, previous=None):
    _, rows, features = held.shape
    rank = sums[0].shape[0]
    chunk = chunk_of(rows, 256)
    slots = 3
    args = [vmem(held), differ, inverse, *sums, *near]
    specs = [in_vmem] * 11
    aliases = {0: 3}
    if previous is not None:
        args.append(hbm(previous))
        specs.append(in_hbm)
        aliases = {0: 3, 11: 0}
    return pl.pallas_call(
        functools.partial(mix_kernel, mat, chunk, slots),
        name=f"mix{mat}",
        out_shape=[
            jax.ShapeDtypeStruct(shape, f32),
            jax.ShapeDtypeStruct((rank, features), f32),
            jax.ShapeDtypeStruct((rank, features), f32),
            jax.ShapeDtypeStruct(held.shape, f32),
        ],
        in_specs=specs,
        out_specs=[in_hbm, in_vmem, in_vmem, in_vmem],
        scratch_shapes=[
            pltpu.VMEM((slots, chunk, features), f32),
            pltpu.SemaphoreType.DMA((slots,)),
        ],
        input_output_aliases=aliases,
        compiler_params=pltpu.CompilerParams(vmem_limit_bytes=8 * mib),
    )(*args)


def exchange(values):
    return [
        shifted(values[1], "rx", -1),
        shifted(values[0], "rx", 1),
        shifted(values[3], "ry", -1),
        shifted(values[2], "ry", 1),
    ]


def per_device(weights, factors_rx, factors_ry):
    mats = weights.shape[2]
    rank = factors_rx.shape[-2]
    factors = [
        factors_rx,
        shifted(factors_rx, "rx", 1),
        factors_ry,
        shifted(factors_ry, "ry", 1),
    ]
    held = load(weights)
    own = []
    for mat in range(mats):
        *own_mat, held = project(held, factors, mat, weights if mat + 1 < mats else None)
        own.append(own_mat)
    near = [exchange(own_mat) for own_mat in own]
    differ, sums, inverse, near_sums = [], [], [], []
    tp = lax.axis_size("tp")
    pairs = []
    for mat in range(mats):
        p, terms, held = back(held, own[mat], near[mat], mat)
        distance = 1
        while 2 * distance < tp:
            terms = terms + from_partner(terms, "tp", distance)
            distance *= 2
        other = from_partner(terms, "tp", distance) if tp > 1 else jnp.zeros_like(terms)
        differ.append(p)
        pairs.append((terms, other))
    grams = []
    for mat in range(mats):
        *sum_mat, gram, held = add(held, *pairs[mat], rank, mat)
        sums.append(sum_mat)
        near_sums.append(exchange(sum_mat))
        grams.append(gram)
    for mat in range(mats):
        factor, held = inverse_factor(held, grams[mat], rank, mat)
        inverse.append(factor)
    mixed = None
    next_rx, next_ry = [], []
    for mat in range(mats):
        mixed, rx, ry, held = mix(
            held,
            differ[mat],
            inverse[mat],
            sums[mat],
            near_sums[mat],
            mat,
            weights.shape,
            mixed,
        )
        next_rx.append(rx)
        next_ry.append(ry)
    return mixed, jnp.stack(next_rx)[None, None], jnp.stack(next_ry)[None, None]


def solution(mesh):
    return jax.shard_map(
        per_device,
        mesh=mesh,
        in_specs=(
            P("rx", "ry", None, "tp", None),
            P("rx", "ry", None, None, None),
            P("rx", "ry", None, None, None),
        ),
        out_specs=(
            P("rx", "ry", None, "tp", None),
            P("rx", "ry", None, None, None),
            P("rx", "ry", None, None, None),
        ),
        check_vma=False,
    )
```

```python
import functools

import jax
import jax.numpy as jnp
from jax import lax
from jax.experimental import pallas as pl
from jax.experimental.pallas import tpu as pltpu
from jax.sharding import PartitionSpec as P

f32 = jnp.float32
bf16 = jnp.bfloat16
mixing = 0.2
edges = 4
mib = 1 << 20

NN = (((1,), (0,)), ((), ()))
NT = (((1,), (1,)), ((), ()))
TN = (((0,), (0,)), ((), ()))

in_vmem = pl.BlockSpec(memory_space=pltpu.VMEM)
in_hbm = pl.BlockSpec(memory_space=pltpu.HBM)


def vmem(value):
    return pltpu.with_memory_space_constraint(value, pltpu.VMEM)


def hbm(value):
    return pltpu.with_memory_space_constraint(value, pltpu.HBM)


def dot(a, b, dims):
    return lax.dot_general(a, b, dims, preferred_element_type=f32)


def split(value):
    high = value.astype(bf16)
    return high, (value - high.astype(f32)).astype(bf16)


def chunk_of(rows, most):
    size = min(rows, most)
    while rows % size:
        size //= 2
    return size


def shifted(value, axis, steps):
    count = lax.axis_size(axis)
    pairs = [(source, (source + steps) % count) for source in range(count)]
    return lax.ppermute(value, axis, pairs)


def from_partner(value, axis, distance):
    count = lax.axis_size(axis)
    return lax.ppermute(value, axis, [(i, i ^ distance) for i in range(count)])


def exchange(values):
    swapped = []
    for slot, value in enumerate(values):
        axis = ("rx", "ry")[slot // 2]
        count = lax.axis_size(axis)
        pairs = [(i, (i + (1 if i % 2 == slot % 2 else -1)) % count) for i in range(count)]
        swapped.append(lax.ppermute(value, axis, pairs))
    return swapped


def odd(axis):
    return lax.rem(lax.axis_index(axis), 2) == 1


def piece_copy(weights, held, sems, size, piece, first):
    rows = held.shape[1]
    mat, row = divmod(piece * size, rows)
    here = pl.ds(row, size)
    return pltpu.make_async_copy(
        weights.at[0, 0, mat, here], held.at[mat, here], sems.at[piece - first]
    )


def load_kernel(size, until, weights, held, sems):
    copies = [piece_copy(weights, held, sems, size, piece, 0) for piece in range(until)]
    for copy in copies:
        copy.start()
    for copy in copies:
        copy.wait()


def load(weights, size, until):
    return pl.pallas_call(
        functools.partial(load_kernel, size, until),
        name="load",
        out_shape=jax.ShapeDtypeStruct(weights.shape[2:], f32),
        in_specs=[in_hbm],
        out_specs=in_vmem,
        scratch_shapes=[pltpu.SemaphoreType.DMA((until,))],
        compiler_params=pltpu.CompilerParams(vmem_limit_bytes=4 * mib),
    )(hbm(weights))


def project_kernel(
    mat, chunk, size, first, until, same, f0, f1, f2, f3, weights, o0, o1, o2, o3, held, sems
):
    rows = held.shape[1]
    copies = {
        piece: piece_copy(weights, held, sems, size, piece, first)
        for piece in range(first, until)
    }
    for copy in copies.values():
        copy.start()
    rank = f0.shape[-2]
    slots = []
    for axis, own, lower in (("rx", f0, f1), ("ry", f2, f3)):
        own, lower, swap = own[0, 0, mat], lower[0, 0, mat], odd(axis)
        slots += [jnp.where(swap, lower, own), jnp.where(swap, own, lower)]
    high, low = split(jnp.concatenate(slots, 0))
    stack = jnp.concatenate(
        [jnp.concatenate([high, high], 1), jnp.concatenate([low, low], 1)], 0
    )
    width = edges * rank
    for row in range(0, rows, chunk):
        here = pl.ds(row, chunk)
        start = mat * rows + row
        for piece in range(start // size, (start + chunk) // size):
            if piece in copies:
                copies.pop(piece).wait()
        w_high, w_low = split(held[mat, here, :])
        both = dot(stack, jnp.concatenate([w_high, w_low], 1), NT)
        total = both[:width] + both[width:]
        for slot, out in enumerate((o0, o1, o2, o3)):
            out[:, here] = total[slot * rank : (slot + 1) * rank]
    for copy in copies.values():
        copy.wait()


def project(held, factors, weights, mat, size, first, until):
    rows = held.shape[1]
    rank = factors[0].shape[-2]
    return pl.pallas_call(
        functools.partial(project_kernel, mat, chunk_of(rows, 1024), size, first, until),
        name=f"project{mat}",
        out_shape=[jax.ShapeDtypeStruct((rank, rows), f32)] * edges
        + [jax.ShapeDtypeStruct(held.shape, f32)],
        in_specs=[in_vmem] * 5 + [in_hbm],
        out_specs=[in_vmem] * (edges + 1),
        scratch_shapes=[pltpu.SemaphoreType.DMA((until - first,))],
        input_output_aliases={0: edges},
        compiler_params=pltpu.CompilerParams(vmem_limit_bytes=4 * mib),
    )(vmem(held), *factors, hbm(weights))


def back_kernel(mat, chunk, same, o0, o1, o2, o3, n0, n1, n2, n3, differ, sums, held):
    rank = o0.shape[0]
    width = edges * rank
    features = held.shape[2]
    sums[...] = jnp.zeros_like(sums)

    def body(step, gram):
        here = pl.ds(pl.multiple_of(step * chunk, chunk), chunk)
        p = jnp.concatenate(
            [o[:, here] - n[:, here] for o, n in zip((o0, o1, o2, o3), (n0, n1, n2, n3))], 0
        )
        differ[:, here] = p
        high, low = split(p)
        w_high, w_low = split(held[mat, here, :])
        pair = jnp.concatenate([high, low], 0)
        stack = jnp.concatenate([pair, pair], 1)
        both = dot(stack, jnp.concatenate([w_high, w_low], 0), NN)
        sums[:, :features] += both[:width] + both[width:]
        return gram + dot(pair, pair, NT)

    gram = lax.fori_loop(
        0, held.shape[1] // chunk, body, jnp.zeros((2 * width, 2 * width), f32)
    )
    total = (gram[:width, :width] + gram[width:, width:]) + (
        gram[:width, width:] + gram[width:, :width]
    )
    for edge in range(edges):
        here = slice(edge * rank, (edge + 1) * rank)
        sums[here, features : features + rank] = total[here, here]


def back(held, own, near, mat):
    _, rows, features = held.shape
    rank = own[0].shape[0]
    return pl.pallas_call(
        functools.partial(back_kernel, mat, chunk_of(rows, 1024)),
        name=f"back{mat}",
        out_shape=[
            jax.ShapeDtypeStruct((edges * rank, rows), f32),
            jax.ShapeDtypeStruct((edges * rank, features + 128), f32),
            jax.ShapeDtypeStruct(held.shape, f32),
        ],
        in_specs=[in_vmem] * 9,
        out_specs=[in_vmem] * 3,
        input_output_aliases={0: 2},
        compiler_params=pltpu.CompilerParams(vmem_limit_bytes=4 * mib),
    )(vmem(held), *own, *near)


def add_kernel(same, mine, other, b0, b1, b2, b3, gram, held):
    rank, features = b0.shape
    for edge, out in enumerate((b0, b1, b2, b3)):
        here = slice(edge * rank, (edge + 1) * rank)
        out[...] = mine[here, :features] + other[here, :features]
    gram[...] = mine[:, features:] + other[:, features:]


def add(held, mine, other, rank, mat):
    width, wide = mine.shape
    features = wide - 128
    return pl.pallas_call(
        add_kernel,
        name=f"add{mat}",
        out_shape=[jax.ShapeDtypeStruct((rank, features), f32)] * edges
        + [jax.ShapeDtypeStruct((width, 128), f32), jax.ShapeDtypeStruct(held.shape, f32)],
        in_specs=[in_vmem] * 3,
        out_specs=[in_vmem] * 6,
        input_output_aliases={0: 5},
        compiler_params=pltpu.CompilerParams(vmem_limit_bytes=4 * mib),
    )(vmem(held), mine, other)


def inverse_kernel(rank, same, *refs):
    count = len(refs) // 2
    grams, inverses = refs[:count], refs[count : 2 * count]
    width = grams[0].shape[0]
    shape = (len(grams) * edges, rank, 128)
    row = lax.broadcasted_iota(jnp.int32, shape, 1)
    lane = lax.broadcasted_iota(jnp.int32, shape, 2)
    slot = lax.rem(lax.broadcasted_iota(jnp.int32, shape, 0), edges)
    value = jnp.concatenate([gram[...] for gram in grams], 0).reshape(shape)
    value = jnp.where(lane < rank, value, (lane == width + slot * rank + row).astype(f32))
    pivots = jnp.ones((shape[0], rank, 1), f32)
    for j in range(rank):
        pivot = value[:, j : j + 1, j : j + 1]
        pivots = jnp.where(row[:, :, :1] == j, pivot, pivots)
        factor = jnp.where(row > j, value[:, :, j : j + 1] / pivot, 0.0)
        value = value - factor * value[:, j : j + 1, :]
    value = (value / jnp.sqrt(pivots)).reshape(len(grams) * width, 128)
    for mat, inverse in enumerate(inverses):
        inverse[...] = value[mat * width : (mat + 1) * width]


def inverse_factors(held, grams, rank):
    return pl.pallas_call(
        functools.partial(inverse_kernel, rank),
        name="inverse",
        out_shape=[jax.ShapeDtypeStruct(gram.shape, f32) for gram in grams]
        + [jax.ShapeDtypeStruct(held.shape, f32)],
        in_specs=[in_vmem] * (len(grams) + 1),
        out_specs=[in_vmem] * (len(grams) + 1),
        input_output_aliases={0: len(grams)},
        compiler_params=pltpu.CompilerParams(vmem_limit_bytes=4 * mib),
    )(vmem(held), *grams)


def mix_kernel(mat, chunk, same, differ, inverse, b0, b1, b2, b3, n0, n1, n2, n3, *rest):
    mixed, next_rx, next_ry, held, new_rx, new_ry, sems, new_sems = rest[-8:]
    rank = b0.shape[0]
    width = edges * rank
    factor = inverse[:, width : 2 * width]
    sums = jnp.concatenate(
        [b[...] + n[...] for b, n in zip((b0, b1, b2, b3), (n0, n1, n2, n3))], 0
    )
    updated = lax.dot_general(
        factor, sums, NN, precision=lax.Precision.HIGHEST, preferred_element_type=f32
    )
    parts = [updated[slot * rank : (slot + 1) * rank] for slot in range(edges)]
    new_rx[...] = jnp.where(odd("rx"), parts[1], parts[0])
    new_ry[...] = jnp.where(odd("ry"), parts[3], parts[2])
    new_copies = [
        pltpu.make_async_copy(new_rx, next_rx.at[0, 0, mat], new_sems.at[0]),
        pltpu.make_async_copy(new_ry, next_ry.at[0, 0, mat], new_sems.at[1]),
    ]
    for copy in new_copies:
        copy.start()
    right = mixing * lax.dot_general(
        factor, updated, TN, precision=lax.Precision.HIGHEST, preferred_element_type=f32
    )
    r_high, r_low = split(right)
    terms = jnp.concatenate([r_high, r_high, r_low, r_low], 0)
    steps = held.shape[1] // chunk

    def copy(step):
        here = pl.ds(pl.multiple_of(step * chunk, chunk), chunk)
        return pltpu.make_async_copy(
            held.at[mat, here], mixed.at[0, 0, mat, here], sems.at[step]
        )

    @pl.loop(0, steps)
    def _(step):
        here = pl.ds(pl.multiple_of(step * chunk, chunk), chunk)
        high, low = split(differ[:, here])
        lhs = jnp.concatenate([high, low, high, low], 0)
        held[mat, here, :] -= dot(lhs, terms, TN)
        copy(step).start()

    @pl.loop(0, steps)
    def _(step):
        copy(step).wait()

    for copy in new_copies:
        copy.wait()


def mix(held, differ, inverse, sums, near, mat, shapes, previous=None):
    _, rows, features = held.shape
    rank = sums[0].shape[0]
    chunk = chunk_of(rows, 256)
    args = [vmem(held), differ, inverse, *sums, *near]
    specs = [in_vmem] * 11
    aliases = {0: 3}
    if previous is not None:
        args += [hbm(array) for array in previous]
        specs += [in_hbm] * 3
        aliases |= {11: 0, 12: 1, 13: 2}
    return pl.pallas_call(
        functools.partial(mix_kernel, mat, chunk),
        name=f"mix{mat}",
        out_shape=[jax.ShapeDtypeStruct(shape, f32) for shape in (*shapes, held.shape)],
        in_specs=specs,
        out_specs=[in_hbm] * 3 + [in_vmem],
        scratch_shapes=[
            pltpu.VMEM((rank, features), f32),
            pltpu.VMEM((rank, features), f32),
            pltpu.SemaphoreType.DMA((rows // chunk,)),
            pltpu.SemaphoreType.DMA((2,)),
        ],
        input_output_aliases=aliases,
        compiler_params=pltpu.CompilerParams(vmem_limit_bytes=4 * mib),
    )(*args)


def per_device(weights, factors_rx, factors_ry):
    mats, rows = weights.shape[2:4]
    rank = factors_rx.shape[-2]
    factors = [
        factors_rx,
        shifted(factors_rx, "rx", 1),
        factors_ry,
        shifted(factors_ry, "ry", 1),
    ]
    size = chunk_of(rows, 512)
    pieces = rows // size
    ahead = max(pieces // 4, 1)
    held = load(weights, size, ahead)
    own = []
    for mat in range(mats):
        first = mat * pieces + ahead
        until = min((mat + 1) * pieces + ahead, mats * pieces)
        *own_mat, held = project(held, factors, weights, mat, size, first, until)
        own.append(own_mat)
    near = [exchange(own_mat) for own_mat in own]
    differ, sums, grams, near_sums, pairs = [], [], [], [], []
    tp = lax.axis_size("tp")
    for mat in range(mats):
        p, terms, held = back(held, own[mat], near[mat], mat)
        distance = 1
        while 2 * distance < tp:
            terms = terms + from_partner(terms, "tp", distance)
            distance *= 2
        other = from_partner(terms, "tp", distance) if tp > 1 else jnp.zeros_like(terms)
        differ.append(p)
        pairs.append((terms, other))
    for mat in range(mats):
        *sum_mat, gram, held = add(held, *pairs[mat], rank, mat)
        sums.append(sum_mat)
        near_sums.append(exchange(sum_mat))
        grams.append(gram)
    *inverse, held = inverse_factors(held, grams, rank)
    results = None
    shapes = (weights.shape, factors_rx.shape, factors_ry.shape)
    for mat in range(mats):
        *results, held = mix(
            held, differ[mat], inverse[mat], sums[mat], near_sums[mat], mat, shapes, results
        )
    return tuple(results)


def solution(mesh):
    return jax.shard_map(
        per_device,
        mesh=mesh,
        in_specs=(
            P("rx", "ry", None, "tp", None),
            P("rx", "ry", None, None, None),
            P("rx", "ry", None, None, None),
        ),
        out_specs=(
            P("rx", "ry", None, "tp", None),
            P("rx", "ry", None, None, None),
            P("rx", "ry", None, None, None),
        ),
        check_vma=False,
    )
```

```python
import functools

import jax
import jax.numpy as jnp
from jax import lax
from jax.experimental import pallas as pl
from jax.experimental.pallas import tpu as pltpu
from jax.sharding import PartitionSpec as P

f32 = jnp.float32
bf16 = jnp.bfloat16
mixing = 0.2
edges = 4
grant = 6 << 20

NN = (((1,), (0,)), ((), ()))
NT = (((1,), (1,)), ((), ()))
TN = (((0,), (0,)), ((), ()))

in_vmem = pl.BlockSpec(memory_space=pltpu.VMEM)
in_hbm = pl.BlockSpec(memory_space=pltpu.HBM)


def vmem(value):
    return pltpu.with_memory_space_constraint(value, pltpu.VMEM)


def hbm(value):
    return pltpu.with_memory_space_constraint(value, pltpu.HBM)


def cost(held, passes):
    _, rows, features = held.shape
    flops = passes * 2 * 256 * rows * features
    return pl.CostEstimate(flops=flops, bytes_accessed=8 * rows * features, transcendentals=0)


def dot(a, b, dims):
    return lax.dot_general(a, b, dims, preferred_element_type=f32)


def split(value):
    high = value.astype(bf16)
    return high, (value - high.astype(f32)).astype(bf16)


def chunk_of(rows, most):
    size = min(rows, most)
    while rows % size:
        size //= 2
    return size


def shifted(value, axis, steps):
    count = lax.axis_size(axis)
    pairs = [(source, (source + steps) % count) for source in range(count)]
    return lax.ppermute(value, axis, pairs)


def from_partner(value, axis, distance):
    count = lax.axis_size(axis)
    return lax.ppermute(value, axis, [(i, i ^ distance) for i in range(count)])


def exchange(values):
    swapped = []
    for slot, value in enumerate(values):
        axis, colour = ("ry", "rx")[slot // 2], 1 - slot % 2
        count = lax.axis_size(axis)
        pairs = [(i, (i + (1 if i % 2 == colour else -1)) % count) for i in range(count)]
        swapped.append(lax.ppermute(value, axis, pairs))
    return swapped


def odd(axis):
    return lax.rem(lax.axis_index(axis), 2) == 1


def piece_copy(weights, held, sems, size, mat, row, sem):
    here = pl.ds(row, size)
    return pltpu.make_async_copy(weights.at[0, 0, mat, here], held.at[mat, here], sems.at[sem])


def piece_copies(weights, held, sems, size, first, until):
    rows = held.shape[1]
    places = [divmod(piece * size, rows) for piece in range(first, until)]
    return [
        piece_copy(weights, held, sems, size, mat, row, sem)
        for sem, (mat, row) in enumerate(places)
    ]


def load_kernel(size, until, weights, held, sems):
    copies = piece_copies(weights, held, sems, size, 0, until)
    for copy in copies:
        copy.start()
    for copy in copies:
        copy.wait()


def load(weights, size, until):
    return pl.pallas_call(
        functools.partial(load_kernel, size, until),
        name="load",
        out_shape=jax.ShapeDtypeStruct(weights.shape[2:], f32),
        in_specs=[in_hbm],
        out_specs=in_vmem,
        scratch_shapes=[pltpu.SemaphoreType.DMA((until,))],
        compiler_params=pltpu.CompilerParams(vmem_limit_bytes=grant),
    )(hbm(weights))


def project_kernel(
    mat, chunk, size, first, until, same, f0, f1, f2, f3, weights, o0, o1, o2, o3, held, sems
):
    rows = held.shape[1]
    pieces = rows // size
    copies = piece_copies(weights, held, sems, size, first, until)
    for copy in copies:
        copy.start()
    rank = f0.shape[-2]
    slots = []
    for axis, own, lower in (("ry", f0, f1), ("rx", f2, f3)):
        own, lower, swap = own[0, 0, mat], lower[0, 0, mat], odd(axis)
        slots += [jnp.where(swap, own, lower), jnp.where(swap, lower, own)]
    high, low = split(jnp.concatenate(slots, 0))
    stack = jnp.concatenate(
        [jnp.concatenate([high, high], 1), jnp.concatenate([low, low], 1)], 0
    )
    width = edges * rank

    @pl.loop(0, rows // chunk)
    def _(step):
        here = pl.ds(pl.multiple_of(step * chunk, chunk), chunk)
        for part in range(chunk // size):
            piece = step * (chunk // size) + part

            @pl.when(mat * pieces + piece >= first)
            def _():
                row = pl.multiple_of(piece * size, size)
                sem = mat * pieces + piece - first
                piece_copy(weights, held, sems, size, mat, row, sem).wait()

        w_high, w_low = split(held[mat, here, :])
        both = dot(stack, jnp.concatenate([w_high, w_low], 1), NT)
        total = both[:width] + both[width:]
        for slot, out in enumerate((o0, o1, o2, o3)):
            out[:, here] = total[slot * rank : (slot + 1) * rank]

    for copy in copies[(mat + 1) * pieces - first :]:
        copy.wait()


def project(held, factors, weights, mat, size, first, until):
    rows = held.shape[1]
    rank = factors[0].shape[-2]
    return pl.pallas_call(
        functools.partial(project_kernel, mat, chunk_of(rows, 1024), size, first, until),
        name=f"project{mat}",
        out_shape=[jax.ShapeDtypeStruct((rank, rows), f32)] * edges
        + [jax.ShapeDtypeStruct(held.shape, f32)],
        in_specs=[in_vmem] * 5 + [in_hbm],
        out_specs=[in_vmem] * (edges + 1),
        scratch_shapes=[pltpu.SemaphoreType.DMA((max(until - first, 1),))],
        input_output_aliases={0: edges},
        cost_estimate=cost(held, 2),
        compiler_params=pltpu.CompilerParams(vmem_limit_bytes=grant),
    )(vmem(held), *factors, hbm(weights))


def back_kernel(mat, chunk, same, o0, o1, o2, o3, n0, n1, n2, n3, differ, sums, held):
    rank = o0.shape[0]
    width = edges * rank
    features = held.shape[2]
    sums[...] = jnp.zeros_like(sums)

    def body(step, gram):
        here = pl.ds(pl.multiple_of(step * chunk, chunk), chunk)
        p = jnp.concatenate(
            [o[:, here] - n[:, here] for o, n in zip((o0, o1, o2, o3), (n0, n1, n2, n3))], 0
        )
        differ[:, here] = p
        high, low = split(p)
        w_high, w_low = split(held[mat, here, :])
        pair = jnp.concatenate([high, low], 0)
        stack = jnp.concatenate([pair, pair], 1)
        both = dot(stack, jnp.concatenate([w_high, w_low], 0), NN)
        sums[:, :features] += both[:width] + both[width:]
        return gram + dot(pair, pair, NT)

    gram = lax.fori_loop(
        0, held.shape[1] // chunk, body, jnp.zeros((2 * width, 2 * width), f32)
    )
    total = (gram[:width, :width] + gram[width:, width:]) + (
        gram[:width, width:] + gram[width:, :width]
    )
    for edge in range(edges):
        here = slice(edge * rank, (edge + 1) * rank)
        sums[here, features : features + rank] = total[here, here]


def back(held, own, near, mat):
    _, rows, features = held.shape
    rank = own[0].shape[0]
    return pl.pallas_call(
        functools.partial(back_kernel, mat, chunk_of(rows, 1024)),
        name=f"back{mat}",
        out_shape=[
            jax.ShapeDtypeStruct((edges * rank, rows), f32),
            jax.ShapeDtypeStruct((edges * rank, features + 128), f32),
            jax.ShapeDtypeStruct(held.shape, f32),
        ],
        in_specs=[in_vmem] * 9,
        out_specs=[in_vmem] * 3,
        input_output_aliases={0: 2},
        cost_estimate=cost(held, 2),
        compiler_params=pltpu.CompilerParams(vmem_limit_bytes=grant),
    )(vmem(held), *own, *near)


def add_kernel(same, *refs):
    *refs, held = refs
    pairs, outs = refs[:-edges], refs[-edges:]
    mats, rank, features = outs[0].shape
    for mat in range(mats):
        mine, other = pairs[2 * mat], pairs[2 * mat + 1]
        for slot, out in enumerate(outs):
            here = slice(slot * rank, (slot + 1) * rank)
            out[mat] = mine[here, :features] + other[here, :features]


def add(held, pairs, rank):
    mats = len(pairs)
    pairs = [terms for pair in pairs for terms in pair]
    sums = jax.ShapeDtypeStruct((mats, rank, held.shape[-1]), f32)
    return pl.pallas_call(
        add_kernel,
        name="add",
        out_shape=[sums] * edges + [jax.ShapeDtypeStruct(held.shape, f32)],
        in_specs=[in_vmem] * (1 + len(pairs)),
        out_specs=[in_vmem] * (edges + 1),
        input_output_aliases={0: edges},
        compiler_params=pltpu.CompilerParams(vmem_limit_bytes=grant),
    )(vmem(held), *pairs)


def inverse_kernel(rank, same, mine, other, inverse, held):
    width = edges * rank
    shape = (edges, rank, 128)
    row = lax.broadcasted_iota(jnp.int32, shape, 1)
    lane = lax.broadcasted_iota(jnp.int32, shape, 2)
    slot = lax.broadcasted_iota(jnp.int32, shape, 0)
    value = (mine[:, -128:] + other[:, -128:]).reshape(shape)
    value = jnp.where(lane < rank, value, (lane == width + slot * rank + row).astype(f32))
    pivots = jnp.ones((edges, rank, 1), f32)
    for j in range(rank):
        pivot = value[:, j : j + 1, j : j + 1]
        pivots = jnp.where(row[:, :, :1] == j, pivot, pivots)
        factor = jnp.where(row > j, value[:, :, j : j + 1] / pivot, 0.0)
        value = value - factor * value[:, j : j + 1, :]
    inverse[...] = (value / jnp.sqrt(pivots)).reshape(width, 128)


def inverse_factor(held, pair, rank, mat):
    return pl.pallas_call(
        functools.partial(inverse_kernel, rank),
        name=f"inverse{mat}",
        out_shape=[
            jax.ShapeDtypeStruct((edges * rank, 128), f32),
            jax.ShapeDtypeStruct(held.shape, f32),
        ],
        in_specs=[in_vmem] * 3,
        out_specs=[in_vmem] * 2,
        input_output_aliases={0: 1},
        compiler_params=pltpu.CompilerParams(vmem_limit_bytes=grant),
    )(vmem(held), *pair)


def mix_kernel(chunk, same, *refs):
    *refs, mixed, next_rx, next_ry, held, new_rx, new_ry, sems, new_sems = refs
    mats, rows, _ = held.shape
    differs, inverses = refs[:mats], refs[mats : 2 * mats]
    sums, near = refs[2 * mats : 2 * mats + edges], refs[2 * mats + edges :]
    rank = sums[0].shape[1]
    width = edges * rank
    steps = rows // chunk

    def copy(mat, step):
        here = pl.ds(pl.multiple_of(step * chunk, chunk), chunk)
        return pltpu.make_async_copy(
            held.at[mat, here], mixed.at[0, 0, mat, here], sems.at[mat, step]
        )

    for mat in range(mats):
        factor = inverses[mat][:, width : 2 * width]
        total = jnp.concatenate([b[mat] + n[mat] for b, n in zip(sums, near)], 0)
        updated = lax.dot_general(
            factor, total, NN, precision=lax.Precision.HIGHEST, preferred_element_type=f32
        )
        parts = [updated[slot * rank : (slot + 1) * rank] for slot in range(edges)]
        new_rx[mat] = jnp.where(odd("rx"), parts[2], parts[3])
        new_ry[mat] = jnp.where(odd("ry"), parts[0], parts[1])
        right = mixing * lax.dot_general(
            factor, updated, TN, precision=lax.Precision.HIGHEST, preferred_element_type=f32
        )
        r_high, r_low = split(right)
        terms = jnp.concatenate([r_high, r_high, r_low, r_low], 0)

        @pl.loop(0, steps)
        def _(step):
            here = pl.ds(pl.multiple_of(step * chunk, chunk), chunk)
            high, low = split(differs[mat][:, here])
            lhs = jnp.concatenate([high, low, high, low], 0)
            held[mat, here, :] -= dot(lhs, terms, TN)
            copy(mat, step).start()

    new_copies = [
        pltpu.make_async_copy(new_rx, next_rx.at[0, 0], new_sems.at[0]),
        pltpu.make_async_copy(new_ry, next_ry.at[0, 0], new_sems.at[1]),
    ]
    for new_copy in new_copies:
        new_copy.start()
    for mat in range(mats):

        @pl.loop(0, steps)
        def _(step):
            copy(mat, step).wait()

    for new_copy in new_copies:
        new_copy.wait()


def mix(held, differs, inverses, sums, near, shapes):
    mats, rows, features = held.shape
    rank = sums[0].shape[1]
    chunk = chunk_of(rows, 512)
    args = [vmem(held), *differs, *inverses, *sums, *near]
    return pl.pallas_call(
        functools.partial(mix_kernel, chunk),
        name="mix",
        out_shape=[jax.ShapeDtypeStruct(shape, f32) for shape in (*shapes, held.shape)],
        in_specs=[in_vmem] * len(args),
        out_specs=[in_hbm] * 3 + [in_vmem],
        scratch_shapes=[
            pltpu.VMEM((mats, rank, features), f32),
            pltpu.VMEM((mats, rank, features), f32),
            pltpu.SemaphoreType.DMA((mats, rows // chunk)),
            pltpu.SemaphoreType.DMA((2,)),
        ],
        input_output_aliases={0: 3},
        cost_estimate=cost(held, 4),
        compiler_params=pltpu.CompilerParams(vmem_limit_bytes=grant),
    )(*args)


def per_device(weights, factors_rx, factors_ry):
    mats, rows = weights.shape[2:4]
    rank = factors_rx.shape[-2]
    lower_ry = shifted(factors_ry, "ry", 1)
    lower_rx = shifted(factors_rx, "rx", 1)
    factors = [factors_ry, lower_ry, factors_rx, lower_rx]
    size = chunk_of(rows, 512)
    pieces = rows // size
    until = max(3 * pieces // 8, 1)
    held = load(weights, size, until)
    own = []
    for mat in range(mats):
        first, until = until, min((mat + 1) * pieces + pieces // 4, mats * pieces)
        *own_mat, held = project(held, factors, weights, mat, size, first, until)
        own.append(own_mat)
    near = [exchange(own_mat) for own_mat in own]
    differs, pairs = [], []
    tp = lax.axis_size("tp")
    for mat in range(mats):
        p, terms, held = back(held, own[mat], near[mat], mat)
        distance = 1
        while 2 * distance < tp:
            terms = terms + from_partner(terms, "tp", distance)
            distance *= 2
        other = from_partner(terms, "tp", distance) if tp > 1 else jnp.zeros_like(terms)
        differs.append(p)
        pairs.append((terms, other))
    inverses = [None] * mats
    for mat in range(mats - 1):
        inverses[mat], held = inverse_factor(held, pairs[mat], rank, mat)
    *sums, held = add(held, pairs, rank)
    near_sums = exchange(sums)
    inverses[-1], held = inverse_factor(held, pairs[-1], rank, mats - 1)
    shapes = (weights.shape, factors_rx.shape, factors_ry.shape)
    *results, held = mix(held, differs, inverses, sums, near_sums, shapes)
    return tuple(results)


def solution(mesh):
    return jax.shard_map(
        per_device,
        mesh=mesh,
        in_specs=(
            P("rx", "ry", None, "tp", None),
            P("rx", "ry", None, None, None),
            P("rx", "ry", None, None, None),
        ),
        out_specs=(
            P("rx", "ry", None, "tp", None),
            P("rx", "ry", None, None, None),
            P("rx", "ry", None, None, None),
        ),
        check_vma=False,
    )
```

```python
import functools

import jax
import jax.numpy as jnp
from jax import lax
from jax.experimental import pallas as pl
from jax.experimental.pallas import tpu as pltpu
from jax.sharding import PartitionSpec as P

f32 = jnp.float32
bf16 = jnp.bfloat16
mixing = 0.2
edges = 4
grant = 6 << 20

NN = (((1,), (0,)), ((), ()))
NT = (((1,), (1,)), ((), ()))
TN = (((0,), (0,)), ((), ()))

in_vmem = pl.BlockSpec(memory_space=pltpu.VMEM)
in_hbm = pl.BlockSpec(memory_space=pltpu.HBM)


def vmem(value):
    return pltpu.with_memory_space_constraint(value, pltpu.VMEM)


def hbm(value):
    return pltpu.with_memory_space_constraint(value, pltpu.HBM)


def cost(held, passes):
    _, rows, features = held.shape
    flops = passes * 2 * 256 * rows * features
    return pl.CostEstimate(flops=flops, bytes_accessed=8 * rows * features, transcendentals=0)


def dot(a, b, dims):
    return lax.dot_general(a, b, dims, preferred_element_type=f32)


def split(value):
    high = value.astype(bf16)
    return high, (value - high.astype(f32)).astype(bf16)


def chunk_of(rows, most):
    size = min(rows, most)
    while rows % size:
        size //= 2
    return size


def shifted(value, axis, steps):
    count = lax.axis_size(axis)
    pairs = [(source, (source + steps) % count) for source in range(count)]
    return lax.ppermute(value, axis, pairs)


def from_partner(value, axis, distance):
    count = lax.axis_size(axis)
    return lax.ppermute(value, axis, [(i, i ^ distance) for i in range(count)])


def exchange(values):
    swapped = []
    for slot, value in enumerate(values):
        axis, colour = ("ry", "rx")[slot // 2], 1 - slot % 2
        count = lax.axis_size(axis)
        pairs = [(i, (i + (1 if i % 2 == colour else -1)) % count) for i in range(count)]
        swapped.append(lax.ppermute(value, axis, pairs))
    return swapped


def odd(axis):
    return lax.rem(lax.axis_index(axis), 2) == 1


def piece_copy(weights, held, sems, size, mat, row, sem):
    here = pl.ds(row, size)
    return pltpu.make_async_copy(weights.at[0, 0, mat, here], held.at[mat, here], sems.at[sem])


def piece_copies(weights, held, sems, size, first, until):
    rows = held.shape[1]
    places = [divmod(piece * size, rows) for piece in range(first, until)]
    return [
        piece_copy(weights, held, sems, size, mat, row, sem)
        for sem, (mat, row) in enumerate(places)
    ]


def load_kernel(size, until, weights, held, sems):
    copies = piece_copies(weights, held, sems, size, 0, until)
    for copy in copies:
        copy.start()
    for copy in copies:
        copy.wait()


def load(weights, size, until):
    return pl.pallas_call(
        functools.partial(load_kernel, size, until),
        name="load",
        out_shape=jax.ShapeDtypeStruct(weights.shape[2:], f32),
        in_specs=[in_hbm],
        out_specs=in_vmem,
        scratch_shapes=[pltpu.SemaphoreType.DMA((until,))],
        compiler_params=pltpu.CompilerParams(vmem_limit_bytes=grant),
    )(hbm(weights))


def project_kernel(
    mat, chunk, size, first, until, same, f0, f1, f2, f3, weights, o0, o1, o2, o3, held, sems
):
    rows = held.shape[1]
    pieces = rows // size
    copies = piece_copies(weights, held, sems, size, first, until)
    for copy in copies:
        copy.start()
    rank = f0.shape[-2]
    slots = []
    for axis, own, lower in (("ry", f0, f1), ("rx", f2, f3)):
        own, lower, swap = own[0, 0, mat], lower[0, 0, mat], odd(axis)
        slots += [jnp.where(swap, own, lower), jnp.where(swap, lower, own)]
    high, low = split(jnp.concatenate(slots, 0))
    stack = jnp.concatenate(
        [jnp.concatenate([high, high], 1), jnp.concatenate([low, low], 1)], 0
    )
    width = edges * rank

    @pl.loop(0, rows // chunk)
    def _(step):
        here = pl.ds(pl.multiple_of(step * chunk, chunk), chunk)
        for part in range(chunk // size):
            piece = step * (chunk // size) + part

            @pl.when(mat * pieces + piece >= first)
            def _():
                row = pl.multiple_of(piece * size, size)
                sem = mat * pieces + piece - first
                piece_copy(weights, held, sems, size, mat, row, sem).wait()

        w_high, w_low = split(held[mat, here, :])
        both = dot(stack, jnp.concatenate([w_high, w_low], 1), NT)
        total = both[:width] + both[width:]
        for slot, out in enumerate((o0, o1, o2, o3)):
            out[:, here] = total[slot * rank : (slot + 1) * rank]

    for copy in copies[(mat + 1) * pieces - first :]:
        copy.wait()


def project(held, factors, weights, mat, size, first, until):
    rows = held.shape[1]
    rank = factors[0].shape[-2]
    return pl.pallas_call(
        functools.partial(project_kernel, mat, chunk_of(rows, 1024), size, first, until),
        name=f"project{mat}",
        out_shape=[jax.ShapeDtypeStruct((rank, rows), f32)] * edges
        + [jax.ShapeDtypeStruct(held.shape, f32)],
        in_specs=[in_vmem] * 5 + [in_hbm],
        out_specs=[in_vmem] * (edges + 1),
        scratch_shapes=[pltpu.SemaphoreType.DMA((max(until - first, 1),))],
        input_output_aliases={0: edges},
        cost_estimate=cost(held, 2),
        compiler_params=pltpu.CompilerParams(vmem_limit_bytes=grant),
    )(vmem(held), *factors, hbm(weights))


def back_kernel(mat, chunk, same, o0, o1, o2, o3, n0, n1, n2, n3, differ, sums, held):
    rank = o0.shape[0]
    width = edges * rank
    features = held.shape[2]
    sums[...] = jnp.zeros_like(sums)

    def body(step, gram):
        here = pl.ds(pl.multiple_of(step * chunk, chunk), chunk)
        p = jnp.concatenate(
            [o[:, here] - n[:, here] for o, n in zip((o0, o1, o2, o3), (n0, n1, n2, n3))], 0
        )
        differ[:, here] = p
        high, low = split(p)
        w_high, w_low = split(held[mat, here, :])
        pair = jnp.concatenate([high, low], 0)
        stack = jnp.concatenate([pair, pair], 1)
        both = dot(stack, jnp.concatenate([w_high, w_low], 0), NN)
        sums[:, :features] += both[:width] + both[width:]
        return gram + dot(pair, pair, NT)

    gram = lax.fori_loop(
        0, held.shape[1] // chunk, body, jnp.zeros((2 * width, 2 * width), f32)
    )
    total = (gram[:width, :width] + gram[width:, width:]) + (
        gram[:width, width:] + gram[width:, :width]
    )
    for edge in range(edges):
        here = slice(edge * rank, (edge + 1) * rank)
        sums[here, features : features + rank] = total[here, here]


def back(held, own, near, mat):
    _, rows, features = held.shape
    rank = own[0].shape[0]
    return pl.pallas_call(
        functools.partial(back_kernel, mat, chunk_of(rows, 1024)),
        name=f"back{mat}",
        out_shape=[
            jax.ShapeDtypeStruct((edges * rank, rows), f32),
            jax.ShapeDtypeStruct((edges * rank, features + 128), f32),
            jax.ShapeDtypeStruct(held.shape, f32),
        ],
        in_specs=[in_vmem] * 9,
        out_specs=[in_vmem] * 3,
        input_output_aliases={0: 2},
        cost_estimate=cost(held, 2),
        compiler_params=pltpu.CompilerParams(vmem_limit_bytes=grant),
    )(vmem(held), *own, *near)


def add_kernel(same, mine, other, *refs):
    *outs, held = refs
    rank, features = outs[0].shape
    for slot, out in enumerate(outs):
        here = slice(slot * rank, (slot + 1) * rank)
        out[...] = mine[here, :features] + other[here, :features]


def add(held, pair, rank, mat):
    sums = jax.ShapeDtypeStruct((rank, held.shape[-1]), f32)
    return pl.pallas_call(
        add_kernel,
        name=f"add{mat}",
        out_shape=[sums] * edges + [jax.ShapeDtypeStruct(held.shape, f32)],
        in_specs=[in_vmem] * 3,
        out_specs=[in_vmem] * (edges + 1),
        input_output_aliases={0: edges},
        compiler_params=pltpu.CompilerParams(vmem_limit_bytes=grant),
    )(vmem(held), *pair)


def inverse_kernel(rank, same, *refs):
    *refs, held = refs
    mats = len(refs) // 3
    width = edges * rank
    shape = (mats * edges, rank, 128)
    row = lax.broadcasted_iota(jnp.int32, shape, 1)
    lane = lax.broadcasted_iota(jnp.int32, shape, 2)
    slot = lax.rem(lax.broadcasted_iota(jnp.int32, shape, 0), edges)
    grams = [refs[2 * mat][:, -128:] + refs[2 * mat + 1][:, -128:] for mat in range(mats)]
    value = jnp.concatenate(grams, 0).reshape(shape)
    value = jnp.where(lane < rank, value, (lane == width + slot * rank + row).astype(f32))
    pivots = jnp.ones((shape[0], rank, 1), f32)
    for j in range(rank):
        pivot = value[:, j : j + 1, j : j + 1]
        pivots = jnp.where(row[:, :, :1] == j, pivot, pivots)
        factor = jnp.where(row > j, value[:, :, j : j + 1] / pivot, 0.0)
        value = value - factor * value[:, j : j + 1, :]
    value = (value / jnp.sqrt(pivots)).reshape(mats * width, 128)
    for mat, inverse in enumerate(refs[2 * mats :]):
        inverse[...] = value[mat * width : (mat + 1) * width]


def inverse_factors(held, pairs, rank):
    mats = len(pairs)
    pairs = [terms for pair in pairs for terms in pair]
    return pl.pallas_call(
        functools.partial(inverse_kernel, rank),
        name="inverse",
        out_shape=[jax.ShapeDtypeStruct((edges * rank, 128), f32)] * mats
        + [jax.ShapeDtypeStruct(held.shape, f32)],
        in_specs=[in_vmem] * (1 + 2 * mats),
        out_specs=[in_vmem] * (1 + mats),
        input_output_aliases={0: mats},
        compiler_params=pltpu.CompilerParams(vmem_limit_bytes=grant),
    )(vmem(held), *pairs)


def mix_kernel(mat, chunk, same, differ, inverse, *refs):
    sums, near = refs[:edges], refs[edges : 2 * edges]
    mixed, next_rx, next_ry, held, new_rx, new_ry, sems, new_sems = refs[-8:]
    rank = sums[0].shape[0]
    width = edges * rank
    steps = held.shape[1] // chunk

    def copy(step):
        here = pl.ds(pl.multiple_of(step * chunk, chunk), chunk)
        return pltpu.make_async_copy(
            held.at[mat, here], mixed.at[0, 0, mat, here], sems.at[step]
        )

    factor = inverse[:, width : 2 * width]
    total = jnp.concatenate([b[...] + n[...] for b, n in zip(sums, near)], 0)
    updated = lax.dot_general(
        factor, total, NN, precision=lax.Precision.HIGHEST, preferred_element_type=f32
    )
    right = mixing * lax.dot_general(
        factor, updated, TN, precision=lax.Precision.HIGHEST, preferred_element_type=f32
    )
    r_high, r_low = split(right)
    terms = jnp.concatenate([r_high, r_high, r_low, r_low], 0)

    @pl.loop(0, steps)
    def _(step):
        here = pl.ds(pl.multiple_of(step * chunk, chunk), chunk)
        high, low = split(differ[:, here])
        lhs = jnp.concatenate([high, low, high, low], 0)
        held[mat, here, :] -= dot(lhs, terms, TN)
        copy(step).start()

    parts = [updated[slot * rank : (slot + 1) * rank] for slot in range(edges)]
    new_rx[...] = jnp.where(odd("rx"), parts[2], parts[3])
    new_ry[...] = jnp.where(odd("ry"), parts[0], parts[1])
    new_copies = [
        pltpu.make_async_copy(new_rx, next_rx.at[0, 0, mat], new_sems.at[0]),
        pltpu.make_async_copy(new_ry, next_ry.at[0, 0, mat], new_sems.at[1]),
    ]
    for new_copy in new_copies:
        new_copy.start()

    @pl.loop(0, steps)
    def _(step):
        copy(step).wait()

    for new_copy in new_copies:
        new_copy.wait()


def mix(held, differ, inverse, sums, near, mat, shapes, previous):
    _, rows, features = held.shape
    rank = sums[0].shape[0]
    chunk = chunk_of(rows, 512)
    args = [vmem(held), differ, inverse, *sums, *near]
    specs = [in_vmem] * len(args) + [in_hbm] * len(previous)
    aliases = {0: 3} | {len(args) + place: place for place in range(len(previous))}
    args += [hbm(array) for array in previous]
    return pl.pallas_call(
        functools.partial(mix_kernel, mat, chunk),
        name=f"mix{mat}",
        out_shape=[jax.ShapeDtypeStruct(shape, f32) for shape in (*shapes, held.shape)],
        in_specs=specs,
        out_specs=[in_hbm] * 3 + [in_vmem],
        scratch_shapes=[
            pltpu.VMEM((rank, features), f32),
            pltpu.VMEM((rank, features), f32),
            pltpu.SemaphoreType.DMA((rows // chunk,)),
            pltpu.SemaphoreType.DMA((2,)),
        ],
        input_output_aliases=aliases,
        cost_estimate=cost(held, 2),
        compiler_params=pltpu.CompilerParams(vmem_limit_bytes=grant),
    )(*args)


def per_device(weights, factors_rx, factors_ry):
    mats, rows = weights.shape[2:4]
    rank = factors_rx.shape[-2]
    lower_ry = shifted(factors_ry, "ry", 1)
    lower_rx = shifted(factors_rx, "rx", 1)
    factors = [factors_ry, lower_ry, factors_rx, lower_rx]
    size = chunk_of(rows, 512)
    pieces = rows // size
    ahead = max(pieces // 2, 1)
    until = ahead
    held = load(weights, size, until)
    own = []
    for mat in range(mats):
        first, until = until, min((mat + 1) * pieces + ahead, mats * pieces)
        *own_mat, held = project(held, factors, weights, mat, size, first, until)
        own.append(own_mat)
    near = [exchange(own_mat) for own_mat in own]
    differs, pairs = [], []
    tp = lax.axis_size("tp")
    for mat in range(mats):
        p, terms, held = back(held, own[mat], near[mat], mat)
        distance = 1
        while 2 * distance < tp:
            terms = terms + from_partner(terms, "tp", distance)
            distance *= 2
        other = from_partner(terms, "tp", distance) if tp > 1 else jnp.zeros_like(terms)
        differs.append(p)
        pairs.append((terms, other))
    sums, near_sums = [], []
    for mat in range(mats):
        *sum_mat, held = add(held, pairs[mat], rank, mat)
        sums.append(sum_mat)
        near_sums.append(exchange(sum_mat))
    *inverses, held = inverse_factors(held, pairs, rank)
    results = []
    shapes = (weights.shape, factors_rx.shape, factors_ry.shape)
    for mat in range(mats):
        *results, held = mix(
            held, differs[mat], inverses[mat], sums[mat], near_sums[mat], mat, shapes, results
        )
    return tuple(results)


def solution(mesh):
    return jax.shard_map(
        per_device,
        mesh=mesh,
        in_specs=(
            P("rx", "ry", None, "tp", None),
            P("rx", "ry", None, None, None),
            P("rx", "ry", None, None, None),
        ),
        out_specs=(
            P("rx", "ry", None, "tp", None),
            P("rx", "ry", None, None, None),
            P("rx", "ry", None, None, None),
        ),
        check_vma=False,
    )
```

```python
import functools

import jax
import jax.numpy as jnp
from jax import lax
from jax.experimental import pallas as pl
from jax.experimental.pallas import tpu as pltpu
from jax.sharding import PartitionSpec as P

f32 = jnp.float32
bf16 = jnp.bfloat16
mixing = 0.2
edges = 4
grant = 6 << 20

NN = (((1,), (0,)), ((), ()))
NT = (((1,), (1,)), ((), ()))
TN = (((0,), (0,)), ((), ()))

in_vmem = pl.BlockSpec(memory_space=pltpu.VMEM)
in_hbm = pl.BlockSpec(memory_space=pltpu.HBM)


def vmem(value):
    return pltpu.with_memory_space_constraint(value, pltpu.VMEM)


def hbm(value):
    return pltpu.with_memory_space_constraint(value, pltpu.HBM)


def cost(held, passes):
    _, rows, features = held.shape
    flops = passes * 2 * 256 * rows * features
    return pl.CostEstimate(flops=flops, bytes_accessed=8 * rows * features, transcendentals=0)


def dot(a, b, dims):
    return lax.dot_general(a, b, dims, preferred_element_type=f32)


def split(value):
    high = value.astype(bf16)
    return high, (value - high.astype(f32)).astype(bf16)


def chunk_of(rows, most):
    size = min(rows, most)
    while rows % size:
        size //= 2
    return size


def shifted(value, axis, steps):
    count = lax.axis_size(axis)
    pairs = [(source, (source + steps) % count) for source in range(count)]
    return lax.ppermute(value, axis, pairs)


def from_partner(value, axis, distance):
    count = lax.axis_size(axis)
    return lax.ppermute(value, axis, [(i, i ^ distance) for i in range(count)])


def swapped(value, slot):
    axis, colour = ("ry", "rx")[slot // 2], 1 - slot % 2
    count = lax.axis_size(axis)
    pairs = [(i, (i + (1 if i % 2 == colour else -1)) % count) for i in range(count)]
    return lax.ppermute(value, axis, pairs)


def odd(axis):
    return lax.rem(lax.axis_index(axis), 2) == 1


def piece_copy(weights, held, sems, size, mat, row, sem):
    here = pl.ds(row, size)
    return pltpu.make_async_copy(weights.at[0, 0, mat, here], held.at[mat, here], sems.at[sem])


def piece_copies(weights, held, sems, size, first, until):
    rows = held.shape[1]
    places = [divmod(piece * size, rows) for piece in range(first, until)]
    return [
        piece_copy(weights, held, sems, size, mat, row, sem)
        for sem, (mat, row) in enumerate(places)
    ]


def load_kernel(size, until, weights, held, sems):
    copies = piece_copies(weights, held, sems, size, 0, until)
    for copy in copies:
        copy.start()
    for copy in copies:
        copy.wait()


def load(weights, size, until):
    return pl.pallas_call(
        functools.partial(load_kernel, size, until),
        name="load",
        out_shape=jax.ShapeDtypeStruct(weights.shape[2:], f32),
        in_specs=[in_hbm],
        out_specs=in_vmem,
        scratch_shapes=[pltpu.SemaphoreType.DMA((until,))],
        compiler_params=pltpu.CompilerParams(vmem_limit_bytes=grant),
    )(hbm(weights))


def project_kernel(
    mat, chunk, size, first, until, same, f0, f1, f2, f3, weights, o0, o1, o2, o3, held, sems
):
    rows = held.shape[1]
    pieces = rows // size
    copies = piece_copies(weights, held, sems, size, first, until)
    for copy in copies:
        copy.start()
    rank = f0.shape[-2]
    slots = []
    for axis, own, lower in (("ry", f0, f1), ("rx", f2, f3)):
        own, lower, swap = own[0, 0, mat], lower[0, 0, mat], odd(axis)
        slots += [jnp.where(swap, own, lower), jnp.where(swap, lower, own)]
    high, low = split(jnp.concatenate(slots, 0))
    stack = jnp.concatenate(
        [jnp.concatenate([high, high], 1), jnp.concatenate([low, low], 1)], 0
    )
    width = edges * rank

    @pl.loop(0, rows // chunk)
    def _(step):
        here = pl.ds(pl.multiple_of(step * chunk, chunk), chunk)
        for part in range(chunk // size):
            piece = step * (chunk // size) + part

            @pl.when(mat * pieces + piece >= first)
            def _():
                row = pl.multiple_of(piece * size, size)
                sem = mat * pieces + piece - first
                piece_copy(weights, held, sems, size, mat, row, sem).wait()

        w_high, w_low = split(held[mat, here, :])
        both = dot(stack, jnp.concatenate([w_high, w_low], 1), NT)
        total = both[:width] + both[width:]
        for slot, out in enumerate((o0, o1, o2, o3)):
            out[:, here] = total[slot * rank : (slot + 1) * rank]

    for copy in copies[(mat + 1) * pieces - first :]:
        copy.wait()


def project(held, factors, weights, mat, size, first, until):
    rows = held.shape[1]
    rank = factors[0].shape[-2]
    return pl.pallas_call(
        functools.partial(project_kernel, mat, chunk_of(rows, 1024), size, first, until),
        name=f"project{mat}",
        out_shape=[jax.ShapeDtypeStruct((rank, rows), f32)] * edges
        + [jax.ShapeDtypeStruct(held.shape, f32)],
        in_specs=[in_vmem] * 5 + [in_hbm],
        out_specs=[in_vmem] * (edges + 1),
        scratch_shapes=[pltpu.SemaphoreType.DMA((max(until - first, 1),))],
        input_output_aliases={0: edges},
        cost_estimate=cost(held, 2),
        compiler_params=pltpu.CompilerParams(vmem_limit_bytes=grant),
    )(vmem(held), *factors, hbm(weights))


def back_kernel(mat, chunk, same, o0, o1, o2, o3, n0, n1, n2, n3, differ, sums, held):
    rank = o0.shape[0]
    width = edges * rank
    features = held.shape[2]
    sums[...] = jnp.zeros_like(sums)

    def body(step, gram):
        here = pl.ds(pl.multiple_of(step * chunk, chunk), chunk)
        p = jnp.concatenate(
            [o[:, here] - n[:, here] for o, n in zip((o0, o1, o2, o3), (n0, n1, n2, n3))], 0
        )
        differ[:, here] = p
        high, low = split(p)
        w_high, w_low = split(held[mat, here, :])
        pair = jnp.concatenate([high, low], 0)
        stack = jnp.concatenate([pair, pair], 1)
        both = dot(stack, jnp.concatenate([w_high, w_low], 0), NN)
        sums[:, :features] += both[:width] + both[width:]
        return gram + dot(pair, pair, NT)

    gram = lax.fori_loop(
        0, held.shape[1] // chunk, body, jnp.zeros((2 * width, 2 * width), f32)
    )
    total = (gram[:width, :width] + gram[width:, width:]) + (
        gram[:width, width:] + gram[width:, :width]
    )
    for edge in range(edges):
        here = slice(edge * rank, (edge + 1) * rank)
        sums[here, features : features + rank] = total[here, here]


def back(held, own, near, mat):
    _, rows, features = held.shape
    rank = own[0].shape[0]
    return pl.pallas_call(
        functools.partial(back_kernel, mat, chunk_of(rows, 1024)),
        name=f"back{mat}",
        out_shape=[
            jax.ShapeDtypeStruct((edges * rank, rows), f32),
            jax.ShapeDtypeStruct((edges * rank, features + 128), f32),
            jax.ShapeDtypeStruct(held.shape, f32),
        ],
        in_specs=[in_vmem] * 9,
        out_specs=[in_vmem] * 3,
        input_output_aliases={0: 2},
        cost_estimate=cost(held, 2),
        compiler_params=pltpu.CompilerParams(vmem_limit_bytes=grant),
    )(vmem(held), *own, *near)


def add_kernel(rank, width, same, *refs):
    count = 2 * width
    pairs, refs = refs[:count], refs[count:-1]
    whole = 4 * (width - 1)
    ends, outs = refs[:whole], refs[whole:]

    def total(mat, slot):
        here = slice(slot * rank, (slot + 1) * rank)
        return pairs[2 * mat][here, :-128] + pairs[2 * mat + 1][here, :-128]

    for slot in range(2):
        outs[slot][...] = total(width - 1, slot)
    for mat in range(width - 1):
        for slot in range(2):
            outs[edges + mat][slot] = ends[4 * mat + slot][...] + ends[4 * mat + 2 + slot][...]
    if len(outs) > 2:
        for slot in range(2, edges):
            for mat in range(width):
                outs[slot][mat] = total(mat, slot)


def add(held, pairs, rank, mat, ends=()):
    mats, _, features = held.shape
    outs = [jax.ShapeDtypeStruct((rank, features), f32)] * 2
    if mat == mats - 1:
        outs = outs + [jax.ShapeDtypeStruct((mats, rank, features), f32)] * 2
        outs = outs + [jax.ShapeDtypeStruct((2, rank, features), f32)] * (mats - 1)
    else:
        pairs = pairs[mat : mat + 1]
    args = [vmem(held), *(terms for pair in pairs for terms in pair), *ends]
    outs = outs + [jax.ShapeDtypeStruct(held.shape, f32)]
    return pl.pallas_call(
        functools.partial(add_kernel, rank, len(pairs)),
        name=f"add{mat}",
        out_shape=outs,
        in_specs=[in_vmem] * len(args),
        out_specs=[in_vmem] * len(outs),
        input_output_aliases={0: len(outs) - 1},
        compiler_params=pltpu.CompilerParams(vmem_limit_bytes=grant),
    )(*args)


def inverse_kernel(rank, same, mine, other, inverse, held):
    width = edges * rank
    shape = (edges, rank, 128)
    row = lax.broadcasted_iota(jnp.int32, shape, 1)
    lane = lax.broadcasted_iota(jnp.int32, shape, 2)
    slot = lax.broadcasted_iota(jnp.int32, shape, 0)
    value = (mine[:, -128:] + other[:, -128:]).reshape(shape)
    value = jnp.where(lane < rank, value, (lane == width + slot * rank + row).astype(f32))
    pivots = jnp.ones((edges, rank, 1), f32)
    for j in range(rank):
        pivot = value[:, j : j + 1, j : j + 1]
        pivots = jnp.where(row[:, :, :1] == j, pivot, pivots)
        factor = jnp.where(row > j, value[:, :, j : j + 1] / pivot, 0.0)
        value = value - factor * value[:, j : j + 1, :]
    inverse[...] = (value / jnp.sqrt(pivots)).reshape(width, 128)


def inverse_factor(held, pair, rank, mat):
    return pl.pallas_call(
        functools.partial(inverse_kernel, rank),
        name=f"inverse{mat}",
        out_shape=[
            jax.ShapeDtypeStruct((edges * rank, 128), f32),
            jax.ShapeDtypeStruct(held.shape, f32),
        ],
        in_specs=[in_vmem] * 3,
        out_specs=[in_vmem] * 2,
        input_output_aliases={0: 1},
        compiler_params=pltpu.CompilerParams(vmem_limit_bytes=grant),
    )(vmem(held), *pair)


def mix_kernel(chunk, same, *refs):
    *refs, mixed, next_rx, next_ry, held, new_rx, new_ry, sems, new_sems = refs
    mats, rows, _ = held.shape
    differs, inverses = refs[:mats], refs[mats : 2 * mats]
    ends = refs[2 * mats :]
    rank = new_rx.shape[1]
    width = edges * rank
    steps = rows // chunk

    def copy(mat, step):
        here = pl.ds(pl.multiple_of(step * chunk, chunk), chunk)
        return pltpu.make_async_copy(
            held.at[mat, here], mixed.at[0, 0, mat, here], sems.at[mat, step]
        )

    done, last, rx_ends = ends[: mats - 1], ends[mats - 1 : mats + 3], ends[mats + 3 :]
    for mat in range(mats):
        factor = inverses[mat][:, width : 2 * width]
        if mat < mats - 1:
            total = [done[mat][0], done[mat][1]]
        else:
            total = [last[0][...] + last[2][...], last[1][...] + last[3][...]]
        total += [rx_ends[0][mat] + rx_ends[2][mat], rx_ends[1][mat] + rx_ends[3][mat]]
        total = jnp.concatenate(total, 0)
        updated = lax.dot_general(
            factor, total, NN, precision=lax.Precision.HIGHEST, preferred_element_type=f32
        )
        parts = [updated[slot * rank : (slot + 1) * rank] for slot in range(edges)]
        new_rx[mat] = jnp.where(odd("rx"), parts[2], parts[3])
        new_ry[mat] = jnp.where(odd("ry"), parts[0], parts[1])
        right = mixing * lax.dot_general(
            factor, updated, TN, precision=lax.Precision.HIGHEST, preferred_element_type=f32
        )
        r_high, r_low = split(right)
        terms = jnp.concatenate([r_high, r_high, r_low, r_low], 0)

        @pl.loop(0, steps)
        def _(step):
            here = pl.ds(pl.multiple_of(step * chunk, chunk), chunk)
            high, low = split(differs[mat][:, here])
            lhs = jnp.concatenate([high, low, high, low], 0)
            held[mat, here, :] -= dot(lhs, terms, TN)
            copy(mat, step).start()

    new_copies = [
        pltpu.make_async_copy(new_rx, next_rx.at[0, 0], new_sems.at[0]),
        pltpu.make_async_copy(new_ry, next_ry.at[0, 0], new_sems.at[1]),
    ]
    for new_copy in new_copies:
        new_copy.start()
    for mat in range(mats):

        @pl.loop(0, steps)
        def _(step):
            copy(mat, step).wait()

    for new_copy in new_copies:
        new_copy.wait()


def mix(held, differs, inverses, ends, rank, shapes):
    mats, rows, features = held.shape
    chunk = chunk_of(rows, 512)
    args = [vmem(held), *differs, *inverses, *ends]
    return pl.pallas_call(
        functools.partial(mix_kernel, chunk),
        name="mix",
        out_shape=[jax.ShapeDtypeStruct(shape, f32) for shape in (*shapes, held.shape)],
        in_specs=[in_vmem] * len(args),
        out_specs=[in_hbm] * 3 + [in_vmem],
        scratch_shapes=[
            pltpu.VMEM((mats, rank, features), f32),
            pltpu.VMEM((mats, rank, features), f32),
            pltpu.SemaphoreType.DMA((mats, rows // chunk)),
            pltpu.SemaphoreType.DMA((2,)),
        ],
        input_output_aliases={0: 3},
        cost_estimate=cost(held, 4),
        compiler_params=pltpu.CompilerParams(vmem_limit_bytes=grant),
    )(*args)


def per_device(weights, factors_rx, factors_ry):
    mats, rows = weights.shape[2:4]
    rank = factors_rx.shape[-2]
    lower_ry = shifted(factors_ry, "ry", 1)
    lower_rx = shifted(factors_rx, "rx", 1)
    factors = [factors_ry, lower_ry, factors_rx, lower_rx]
    size = chunk_of(rows, 512)
    pieces = rows // size
    ahead = max(pieces // 2, 1)
    until = ahead
    held = load(weights, size, until)
    own, near = [], []
    for mat in range(mats):
        first, until = until, min((mat + 1) * pieces + ahead, mats * pieces)
        *own_mat, held = project(held, factors, weights, mat, size, first, until)
        own.append(own_mat)
        near.append([swapped(value, slot) for slot, value in enumerate(own_mat)])
    differs, pairs = [], []
    tp = lax.axis_size("tp")
    for mat in range(mats):
        p, terms, held = back(held, own[mat], near[mat], mat)
        distance = 1
        while 2 * distance < tp:
            terms = terms + from_partner(terms, "tp", distance)
            distance *= 2
        other = from_partner(terms, "tp", distance) if tp > 1 else jnp.zeros_like(terms)
        differs.append(p)
        pairs.append((terms, other))
    inverses, ends = [], []
    for mat in range(mats - 1):
        *sums, held = add(held, pairs, rank, mat)
        ends += [*sums, *(swapped(value, slot) for slot, value in enumerate(sums))]
        inverse, held = inverse_factor(held, pairs[mat], rank, mat)
        inverses.append(inverse)
    *sums, held = add(held, pairs, rank, mats - 1, ends)
    sums, done = sums[:edges], sums[edges:]
    near_sums = [swapped(value, slot) for slot, value in enumerate(sums)]
    ends = [*done, *sums[:2], *near_sums[:2], *sums[2:], *near_sums[2:]]
    inverse, held = inverse_factor(held, pairs[-1], rank, mats - 1)
    inverses.append(inverse)
    shapes = (weights.shape, factors_rx.shape, factors_ry.shape)
    *results, held = mix(held, differs, inverses, ends, rank, shapes)
    return tuple(results)


def solution(mesh):
    return jax.shard_map(
        per_device,
        mesh=mesh,
        in_specs=(
            P("rx", "ry", None, "tp", None),
            P("rx", "ry", None, None, None),
            P("rx", "ry", None, None, None),
        ),
        out_specs=(
            P("rx", "ry", None, "tp", None),
            P("rx", "ry", None, None, None),
            P("rx", "ry", None, None, None),
        ),
        check_vma=False,
    )
```

```python
import functools

import jax
import jax.numpy as jnp
from jax import lax
from jax.experimental import pallas as pl
from jax.experimental.pallas import tpu as pltpu
from jax.sharding import PartitionSpec as P

f32 = jnp.float32
bf16 = jnp.bfloat16
mixing = 0.2
edges = 4
grant = 8 << 20

NN = (((1,), (0,)), ((), ()))
NT = (((1,), (1,)), ((), ()))
TN = (((0,), (0,)), ((), ()))

in_vmem = pl.BlockSpec(memory_space=pltpu.VMEM)
in_hbm = pl.BlockSpec(memory_space=pltpu.HBM)


def vmem(value):
    return pltpu.with_memory_space_constraint(value, pltpu.VMEM)


def hbm(value):
    return pltpu.with_memory_space_constraint(value, pltpu.HBM)


def cost(held, passes):
    _, rows, features = held.shape
    flops = passes * 2 * 256 * rows * features
    return pl.CostEstimate(flops=flops, bytes_accessed=8 * rows * features, transcendentals=0)


def dot(a, b, dims):
    return lax.dot_general(a, b, dims, preferred_element_type=f32)


def split(value):
    high = value.astype(bf16)
    return high, (value - high.astype(f32)).astype(bf16)


def chunk_of(rows, most):
    size = min(rows, most)
    while rows % size:
        size //= 2
    return size


def shifted(value, axis, steps):
    count = lax.axis_size(axis)
    pairs = [(source, (source + steps) % count) for source in range(count)]
    return lax.ppermute(value, axis, pairs)


def from_partner(value, axis, distance):
    count = lax.axis_size(axis)
    return lax.ppermute(value, axis, [(i, i ^ distance) for i in range(count)])


def exchange(values):
    swapped = []
    for slot, value in enumerate(values):
        axis, colour = ("ry", "rx")[slot // 2], 1 - slot % 2
        count = lax.axis_size(axis)
        pairs = [(i, (i + (1 if i % 2 == colour else -1)) % count) for i in range(count)]
        swapped.append(lax.ppermute(value, axis, pairs))
    return swapped


def odd(axis):
    return lax.rem(lax.axis_index(axis), 2) == 1


def piece_copy(weights, held, sems, size, mat, row, sem):
    here = pl.ds(row, size)
    return pltpu.make_async_copy(weights.at[0, 0, mat, here], held.at[mat, here], sems.at[sem])


def piece_copies(weights, held, sems, size, first, until):
    rows = held.shape[1]
    places = [divmod(piece * size, rows) for piece in range(first, until)]
    return [
        piece_copy(weights, held, sems, size, mat, row, sem)
        for sem, (mat, row) in enumerate(places)
    ]


def load_kernel(size, until, weights, held, sems):
    copies = piece_copies(weights, held, sems, size, 0, until)
    for copy in copies:
        copy.start()
    for copy in copies:
        copy.wait()


def load(weights, size, until):
    return pl.pallas_call(
        functools.partial(load_kernel, size, until),
        name="load",
        out_shape=jax.ShapeDtypeStruct(weights.shape[2:], f32),
        in_specs=[in_hbm],
        out_specs=in_vmem,
        scratch_shapes=[pltpu.SemaphoreType.DMA((until,))],
        compiler_params=pltpu.CompilerParams(vmem_limit_bytes=grant),
    )(hbm(weights))


def project_kernel(
    mat, chunk, size, first, until, same, f0, f1, f2, f3, weights, o0, o1, o2, o3, held, sems
):
    rows = held.shape[1]
    pieces = rows // size
    copies = piece_copies(weights, held, sems, size, first, until)
    for copy in copies:
        copy.start()
    rank = f0.shape[-2]
    slots = []
    for axis, own, lower in (("ry", f0, f1), ("rx", f2, f3)):
        own, lower, swap = own[0, 0, mat], lower[0, 0, mat], odd(axis)
        slots += [jnp.where(swap, own, lower), jnp.where(swap, lower, own)]
    high, low = split(jnp.concatenate(slots, 0))
    stack = jnp.concatenate(
        [jnp.concatenate([high, high], 1), jnp.concatenate([low, low], 1)], 0
    )
    width = edges * rank

    @pl.loop(0, rows // chunk)
    def _(step):
        here = pl.ds(pl.multiple_of(step * chunk, chunk), chunk)
        for part in range(chunk // size):
            piece = step * (chunk // size) + part

            @pl.when(mat * pieces + piece >= first)
            def _():
                row = pl.multiple_of(piece * size, size)
                sem = mat * pieces + piece - first
                piece_copy(weights, held, sems, size, mat, row, sem).wait()

        w_high, w_low = split(held[mat, here, :])
        both = dot(stack, jnp.concatenate([w_high, w_low], 1), NT)
        total = both[:width] + both[width:]
        for slot, out in enumerate((o0, o1, o2, o3)):
            out[:, here] = total[slot * rank : (slot + 1) * rank]

    for copy in copies[(mat + 1) * pieces - first :]:
        copy.wait()


def project(held, factors, weights, mat, size, first, until):
    rows = held.shape[1]
    rank = factors[0].shape[-2]
    return pl.pallas_call(
        functools.partial(project_kernel, mat, chunk_of(rows, 1024), size, first, until),
        name=f"project{mat}",
        out_shape=[jax.ShapeDtypeStruct((rank, rows), f32)] * edges
        + [jax.ShapeDtypeStruct(held.shape, f32)],
        in_specs=[in_vmem] * 5 + [in_hbm],
        out_specs=[in_vmem] * (edges + 1),
        scratch_shapes=[pltpu.SemaphoreType.DMA((max(until - first, 1),))],
        input_output_aliases={0: edges},
        cost_estimate=cost(held, 2),
        compiler_params=pltpu.CompilerParams(vmem_limit_bytes=grant),
    )(vmem(held), *factors, hbm(weights))


def back_kernel(mat, chunk, same, o0, o1, o2, o3, n0, n1, n2, n3, differ, sums, held):
    rank = o0.shape[0]
    width = edges * rank
    features = held.shape[2]
    sums[...] = jnp.zeros_like(sums)

    def body(step, gram):
        here = pl.ds(pl.multiple_of(step * chunk, chunk), chunk)
        p = jnp.concatenate(
            [o[:, here] - n[:, here] for o, n in zip((o0, o1, o2, o3), (n0, n1, n2, n3))], 0
        )
        differ[:, here] = p
        high, low = split(p)
        w_high, w_low = split(held[mat, here, :])
        pair = jnp.concatenate([high, low], 0)
        stack = jnp.concatenate([pair, pair], 1)
        both = dot(stack, jnp.concatenate([w_high, w_low], 0), NN)
        sums[:, :features] += both[:width] + both[width:]
        return gram + dot(pair, pair, NT)

    gram = lax.fori_loop(
        0, held.shape[1] // chunk, body, jnp.zeros((2 * width, 2 * width), f32)
    )
    total = (gram[:width, :width] + gram[width:, width:]) + (
        gram[:width, width:] + gram[width:, :width]
    )
    for edge in range(edges):
        here = slice(edge * rank, (edge + 1) * rank)
        sums[here, features : features + rank] = total[here, here]


def back(held, own, near, mat):
    _, rows, features = held.shape
    rank = own[0].shape[0]
    return pl.pallas_call(
        functools.partial(back_kernel, mat, chunk_of(rows, 4096)),
        name=f"back{mat}",
        out_shape=[
            jax.ShapeDtypeStruct((edges * rank, rows), f32),
            jax.ShapeDtypeStruct((edges * rank, features + 128), f32),
            jax.ShapeDtypeStruct(held.shape, f32),
        ],
        in_specs=[in_vmem] * 9,
        out_specs=[in_vmem] * 3,
        input_output_aliases={0: 2},
        cost_estimate=cost(held, 2),
        compiler_params=pltpu.CompilerParams(vmem_limit_bytes=grant),
    )(vmem(held), *own, *near)


def add_kernel(same, mine, other, *refs):
    *outs, held = refs
    rank, features = outs[0].shape
    for slot, out in enumerate(outs):
        here = slice(slot * rank, (slot + 1) * rank)
        out[...] = mine[here, :features] + other[here, :features]


def add(held, pair, rank, mat):
    sums = jax.ShapeDtypeStruct((rank, held.shape[-1]), f32)
    return pl.pallas_call(
        add_kernel,
        name=f"add{mat}",
        out_shape=[sums] * edges + [jax.ShapeDtypeStruct(held.shape, f32)],
        in_specs=[in_vmem] * 3,
        out_specs=[in_vmem] * (edges + 1),
        input_output_aliases={0: edges},
        compiler_params=pltpu.CompilerParams(vmem_limit_bytes=grant),
    )(vmem(held), *pair)


def inverse_of(gram, rank):
    width = edges * rank
    shape = (edges, rank, 128)
    row = lax.broadcasted_iota(jnp.int32, shape, 1)
    lane = lax.broadcasted_iota(jnp.int32, shape, 2)
    slot = lax.broadcasted_iota(jnp.int32, shape, 0)
    value = gram.reshape(shape)
    value = jnp.where(lane < rank, value, (lane == width + slot * rank + row).astype(f32))
    pivots = jnp.ones((edges, rank, 1), f32)
    for j in range(rank):
        pivot = value[:, j : j + 1, j : j + 1]
        pivots = jnp.where(row[:, :, :1] == j, pivot, pivots)
        factor = jnp.where(row > j, value[:, :, j : j + 1] / pivot, 0.0)
        value = value - factor * value[:, j : j + 1, :]
    return (value / jnp.sqrt(pivots)).reshape(width, 128)


def inverse_kernel(rank, same, mine, other, inverse, held):
    inverse[...] = inverse_of(mine[:, -128:] + other[:, -128:], rank)


def inverse_factor(held, pair, rank):
    return pl.pallas_call(
        functools.partial(inverse_kernel, rank),
        name="inverse",
        out_shape=[
            jax.ShapeDtypeStruct((edges * rank, 128), f32),
            jax.ShapeDtypeStruct(held.shape, f32),
        ],
        in_specs=[in_vmem] * 3,
        out_specs=[in_vmem] * 2,
        input_output_aliases={0: 1},
        compiler_params=pltpu.CompilerParams(vmem_limit_bytes=grant),
    )(vmem(held), *pair)


def mix_kernel(mat, chunk, late, same, differ, inverse, *refs):
    sums, near = refs[:edges], refs[edges : 2 * edges]
    mixed, next_rx, next_ry, held, following, new_rx, new_ry, sems, new_sems = refs[-9:]
    rank = sums[0].shape[0]
    width = edges * rank
    mats, rows, _ = held.shape
    steps = rows // chunk
    mine = steps - (late if mat < mats - 1 else 0)

    def copy(which, row, size, sem):
        here = pl.ds(row, size)
        return pltpu.make_async_copy(
            held.at[which, here], mixed.at[0, 0, which, here], sems.at[sem]
        )

    left = [copy(mat - 1, rows - late * chunk, late * chunk, steps)] if mat and late else []
    for other in left:
        other.start()
    factor = inverse[:, width : 2 * width]
    total = jnp.concatenate([b[...] + n[...] for b, n in zip(sums, near)], 0)
    updated = lax.dot_general(
        factor, total, NN, precision=lax.Precision.HIGHEST, preferred_element_type=f32
    )
    right = mixing * lax.dot_general(
        factor, updated, TN, precision=lax.Precision.HIGHEST, preferred_element_type=f32
    )
    r_high, r_low = split(right)
    terms = jnp.concatenate([r_high, r_high, r_low, r_low], 0)

    def correct(row, size):
        here = pl.ds(row, size)
        high, low = split(differ[:, here])
        lhs = jnp.concatenate([high, low, high, low], 0)
        held[mat, here, :] -= dot(lhs, terms, TN)

    halves = [copy(mat, 0, chunk // 2, 0), copy(mat, chunk // 2, chunk // 2, steps + 1)]
    for half in range(2):
        correct(half * (chunk // 2), chunk // 2)
        halves[half].start()

    def place(step):
        return pl.multiple_of(step * chunk, chunk)

    @pl.loop(1, mine)
    def _(step):
        correct(place(step), chunk)
        copy(mat, place(step), chunk, step).start()

    @pl.loop(mine, steps)
    def _(step):
        correct(place(step), chunk)

    parts = [updated[slot * rank : (slot + 1) * rank] for slot in range(edges)]
    new_rx[...] = jnp.where(odd("rx"), parts[2], parts[3])
    new_ry[...] = jnp.where(odd("ry"), parts[0], parts[1])
    new_copies = [
        pltpu.make_async_copy(new_rx, next_rx.at[0, 0, mat], new_sems.at[0]),
        pltpu.make_async_copy(new_ry, next_ry.at[0, 0, mat], new_sems.at[1]),
    ]
    for new_copy in new_copies:
        new_copy.start()
    if mat < mats - 1:
        gram, gram_other = refs[2 * edges : 2 * edges + 2]
        following[...] = inverse_of(gram[:, -128:] + gram_other[:, -128:], rank)
    else:
        following[...] = inverse[...]
    for half in halves:
        half.wait()

    @pl.loop(1, mine)
    def _(step):
        copy(mat, place(step), chunk, step).wait()

    for other in left + new_copies:
        other.wait()


def mix(held, differ, inverse, sums, near, mat, shapes, pair, previous):
    mats, rows, features = held.shape
    rank = sums[0].shape[0]
    chunk = chunk_of(rows, 512)
    steps = rows // chunk
    args = [vmem(held), differ, inverse, *sums, *near, *pair]
    specs = [in_vmem] * len(args) + [in_hbm] * len(previous)
    aliases = {0: 3} | {len(args) + place: place for place in range(len(previous))}
    args += [hbm(array) for array in previous]
    shapes = (*shapes, held.shape, inverse.shape)
    return pl.pallas_call(
        functools.partial(mix_kernel, mat, chunk, 3 * steps // 8),
        name=f"mix{mat}",
        out_shape=[jax.ShapeDtypeStruct(shape, f32) for shape in shapes],
        in_specs=specs,
        out_specs=[in_hbm] * 3 + [in_vmem] * 2,
        scratch_shapes=[
            pltpu.VMEM((rank, features), f32),
            pltpu.VMEM((rank, features), f32),
            pltpu.SemaphoreType.DMA((steps + 2,)),
            pltpu.SemaphoreType.DMA((2,)),
        ],
        input_output_aliases=aliases,
        cost_estimate=cost(held, 2),
        compiler_params=pltpu.CompilerParams(vmem_limit_bytes=grant),
    )(*args)


def per_device(weights, factors_rx, factors_ry):
    mats, rows = weights.shape[2:4]
    rank = factors_rx.shape[-2]
    lower_ry = shifted(factors_ry, "ry", 1)
    lower_rx = shifted(factors_rx, "rx", 1)
    factors = [factors_ry, lower_ry, factors_rx, lower_rx]
    size = chunk_of(rows, 512)
    pieces = rows // size
    ahead = max(pieces // 2, 1)
    until = ahead
    held = load(weights, size, until)
    own = []
    for mat in range(mats):
        first, until = until, min((mat + 1) * pieces + ahead, mats * pieces)
        *own_mat, held = project(held, factors, weights, mat, size, first, until)
        own.append(own_mat)
    near = [exchange(own_mat) for own_mat in own]
    differs, pairs = [], []
    tp = lax.axis_size("tp")
    for mat in range(mats):
        p, terms, held = back(held, own[mat], near[mat], mat)
        distance = 1
        while 2 * distance < tp:
            terms = terms + from_partner(terms, "tp", distance)
            distance *= 2
        other = from_partner(terms, "tp", distance) if tp > 1 else jnp.zeros_like(terms)
        differs.append(p)
        pairs.append((terms, other))
    sums, near_sums = [], []
    for mat in range(mats):
        *sum_mat, held = add(held, pairs[mat], rank, mat)
        sums.append(sum_mat)
        near_sums.append(exchange(sum_mat))
        if mat == 0:
            inverse, held = inverse_factor(held, pairs[0], rank)
    results = []
    shapes = (weights.shape, factors_rx.shape, factors_ry.shape)
    for mat in range(mats):
        pair = pairs[mat + 1] if mat + 1 < mats else ()
        *results, held, inverse = mix(
            held, differs[mat], inverse, sums[mat], near_sums[mat], mat, shapes, pair, results
        )
    return tuple(results)


def solution(mesh):
    return jax.shard_map(
        per_device,
        mesh=mesh,
        in_specs=(
            P("rx", "ry", None, "tp", None),
            P("rx", "ry", None, None, None),
            P("rx", "ry", None, None, None),
        ),
        out_specs=(
            P("rx", "ry", None, "tp", None),
            P("rx", "ry", None, None, None),
            P("rx", "ry", None, None, None),
        ),
        check_vma=False,
    )
```

```python
import functools

import jax
import jax.numpy as jnp
from jax import lax
from jax.experimental import pallas as pl
from jax.experimental.pallas import tpu as pltpu
from jax.sharding import PartitionSpec as P

f32 = jnp.float32
bf16 = jnp.bfloat16
mixing = 0.2
edges = 4
grant = 8 << 20

NN = (((1,), (0,)), ((), ()))
NT = (((1,), (1,)), ((), ()))
TN = (((0,), (0,)), ((), ()))

in_vmem = pl.BlockSpec(memory_space=pltpu.VMEM)
in_hbm = pl.BlockSpec(memory_space=pltpu.HBM)


def vmem(value):
    return pltpu.with_memory_space_constraint(value, pltpu.VMEM)


def hbm(value):
    return pltpu.with_memory_space_constraint(value, pltpu.HBM)


def cost(held, passes):
    _, rows, features = held.shape
    flops = passes * 2 * 256 * rows * features
    return pl.CostEstimate(flops=flops, bytes_accessed=8 * rows * features, transcendentals=0)


def dot(a, b, dims):
    return lax.dot_general(a, b, dims, preferred_element_type=f32)


def split(value):
    high = value.astype(bf16)
    return high, (value - high.astype(f32)).astype(bf16)


def chunk_of(rows, most):
    size = min(rows, most)
    while rows % size:
        size //= 2
    return size


def chunks_of(rows, size):
    if rows % (4 * size):
        return [(0, rows)]
    return [(0, rows // 2), (rows // 2, rows // 4), (3 * rows // 4, rows // 4)]


def shifted(value, axis, steps):
    count = lax.axis_size(axis)
    pairs = [(source, (source + steps) % count) for source in range(count)]
    return lax.ppermute(value, axis, pairs)


def from_partner(value, axis, distance):
    count = lax.axis_size(axis)
    return lax.ppermute(value, axis, [(i, i ^ distance) for i in range(count)])


def exchange(values):
    swapped = []
    for slot, value in enumerate(values):
        axis, colour = ("ry", "rx")[slot // 2], 1 - slot % 2
        count = lax.axis_size(axis)
        pairs = [(i, (i + (1 if i % 2 == colour else -1)) % count) for i in range(count)]
        swapped.append(lax.ppermute(value, axis, pairs))
    return swapped


def odd(axis):
    return lax.rem(lax.axis_index(axis), 2) == 1


def piece_copy(weights, held, sems, size, mat, row, sem):
    here = pl.ds(row, size)
    return pltpu.make_async_copy(weights.at[0, 0, mat, here], held.at[mat, here], sems.at[sem])


def piece_copies(weights, held, sems, size, first, until):
    rows = held.shape[1]
    places = [divmod(piece * size, rows) for piece in range(first, until)]
    return [
        piece_copy(weights, held, sems, size, mat, row, sem)
        for sem, (mat, row) in enumerate(places)
    ]


def load_kernel(size, until, weights, held, sems):
    copies = piece_copies(weights, held, sems, size, 0, until)
    for copy in copies:
        copy.start()
    for copy in copies:
        copy.wait()


def load(weights, size, until):
    return pl.pallas_call(
        functools.partial(load_kernel, size, until),
        name="load",
        out_shape=jax.ShapeDtypeStruct(weights.shape[2:], f32),
        in_specs=[in_hbm],
        out_specs=in_vmem,
        scratch_shapes=[pltpu.SemaphoreType.DMA((until,))],
        compiler_params=pltpu.CompilerParams(vmem_limit_bytes=grant),
    )(hbm(weights))


def project_kernel(
    mat, chunk, size, first, until, same, f0, f1, f2, f3, weights, o0, o1, o2, o3, held, sems
):
    rows = held.shape[1]
    pieces = rows // size
    copies = piece_copies(weights, held, sems, size, first, until)
    for copy in copies:
        copy.start()
    rank = f0.shape[-2]
    slots = []
    for axis, own, lower in (("ry", f0, f1), ("rx", f2, f3)):
        own, lower, swap = own[0, 0, mat], lower[0, 0, mat], odd(axis)
        slots += [jnp.where(swap, own, lower), jnp.where(swap, lower, own)]
    high, low = split(jnp.concatenate(slots, 0))
    stack = jnp.concatenate(
        [jnp.concatenate([high, high], 1), jnp.concatenate([low, low], 1)], 0
    )
    width = edges * rank

    @pl.loop(0, rows // chunk)
    def _(step):
        here = pl.ds(pl.multiple_of(step * chunk, chunk), chunk)
        for part in range(chunk // size):
            piece = step * (chunk // size) + part

            @pl.when(mat * pieces + piece >= first)
            def _():
                row = pl.multiple_of(piece * size, size)
                sem = mat * pieces + piece - first
                piece_copy(weights, held, sems, size, mat, row, sem).wait()

        w_high, w_low = split(held[mat, here, :])
        both = dot(stack, jnp.concatenate([w_high, w_low], 1), NT)
        total = both[:width] + both[width:]
        for slot, out in enumerate((o0, o1, o2, o3)):
            out[:, here] = total[slot * rank : (slot + 1) * rank]

    for copy in copies[(mat + 1) * pieces - first :]:
        copy.wait()


def project(held, factors, weights, mat, size, first, until):
    rows = held.shape[1]
    rank = factors[0].shape[-2]
    return pl.pallas_call(
        functools.partial(project_kernel, mat, chunk_of(rows, 1024), size, first, until),
        name=f"project{mat}",
        out_shape=[jax.ShapeDtypeStruct((rank, rows), f32)] * edges
        + [jax.ShapeDtypeStruct(held.shape, f32)],
        in_specs=[in_vmem] * 5 + [in_hbm],
        out_specs=[in_vmem] * (edges + 1),
        scratch_shapes=[pltpu.SemaphoreType.DMA((max(until - first, 1),))],
        input_output_aliases={0: edges},
        cost_estimate=cost(held, 2),
        compiler_params=pltpu.CompilerParams(vmem_limit_bytes=grant),
    )(vmem(held), *factors, hbm(weights))


def back_kernel(mat, chunk, same, o0, o1, o2, o3, n0, n1, n2, n3, differ, sums, held):
    rank = o0.shape[0]
    width = edges * rank
    features = held.shape[2]
    sums[...] = jnp.zeros_like(sums)

    def body(step, gram):
        here = pl.ds(pl.multiple_of(step * chunk, chunk), chunk)
        p = jnp.concatenate(
            [o[:, here] - n[:, here] for o, n in zip((o0, o1, o2, o3), (n0, n1, n2, n3))], 0
        )
        differ[:, here] = p
        high, low = split(p)
        w_high, w_low = split(held[mat, here, :])
        pair = jnp.concatenate([high, low], 0)
        stack = jnp.concatenate([pair, pair], 1)
        both = dot(stack, jnp.concatenate([w_high, w_low], 0), NN)
        sums[:, :features] += both[:width] + both[width:]
        return gram + dot(pair, pair, NT)

    gram = lax.fori_loop(
        0, held.shape[1] // chunk, body, jnp.zeros((2 * width, 2 * width), f32)
    )
    total = (gram[:width, :width] + gram[width:, width:]) + (
        gram[:width, width:] + gram[width:, :width]
    )
    for edge in range(edges):
        here = slice(edge * rank, (edge + 1) * rank)
        sums[here, features : features + rank] = total[here, here]


def back(held, own, near, mat):
    _, rows, features = held.shape
    rank = own[0].shape[0]
    return pl.pallas_call(
        functools.partial(back_kernel, mat, chunk_of(rows, 4096)),
        name=f"back{mat}",
        out_shape=[
            jax.ShapeDtypeStruct((edges * rank, rows), f32),
            jax.ShapeDtypeStruct((edges * rank, features + 128), f32),
            jax.ShapeDtypeStruct(held.shape, f32),
        ],
        in_specs=[in_vmem] * 9,
        out_specs=[in_vmem] * 3,
        input_output_aliases={0: 2},
        cost_estimate=cost(held, 2),
        compiler_params=pltpu.CompilerParams(vmem_limit_bytes=grant),
    )(vmem(held), *own, *near)


def add_kernel(same, mine, other, *refs):
    *outs, held = refs
    rank, features = outs[0].shape
    for slot, out in enumerate(outs):
        here = slice(slot * rank, (slot + 1) * rank)
        out[...] = mine[here, :features] + other[here, :features]


def add(held, pair, rank, mat):
    sums = jax.ShapeDtypeStruct((rank, held.shape[-1]), f32)
    return pl.pallas_call(
        add_kernel,
        name=f"add{mat}",
        out_shape=[sums] * edges + [jax.ShapeDtypeStruct(held.shape, f32)],
        in_specs=[in_vmem] * 3,
        out_specs=[in_vmem] * (edges + 1),
        input_output_aliases={0: edges},
        compiler_params=pltpu.CompilerParams(vmem_limit_bytes=grant),
    )(vmem(held), *pair)


def inverse_of(gram, rank):
    width = edges * rank
    shape = (edges, rank, 128)
    row = lax.broadcasted_iota(jnp.int32, shape, 1)
    lane = lax.broadcasted_iota(jnp.int32, shape, 2)
    slot = lax.broadcasted_iota(jnp.int32, shape, 0)
    value = gram.reshape(shape)
    value = jnp.where(lane < rank, value, (lane == width + slot * rank + row).astype(f32))
    pivots = jnp.ones((edges, rank, 1), f32)
    for j in range(rank):
        pivot = value[:, j : j + 1, j : j + 1]
        pivots = jnp.where(row[:, :, :1] == j, pivot, pivots)
        factor = jnp.where(row > j, value[:, :, j : j + 1] / pivot, 0.0)
        value = value - factor * value[:, j : j + 1, :]
    return (value / jnp.sqrt(pivots)).reshape(width, 128)


def inverse_kernel(rank, same, mine, other, inverse, held):
    inverse[...] = inverse_of(mine[:, -128:] + other[:, -128:], rank)


def inverse_factor(held, pair, rank):
    return pl.pallas_call(
        functools.partial(inverse_kernel, rank),
        name="inverse",
        out_shape=[
            jax.ShapeDtypeStruct((edges * rank, 128), f32),
            jax.ShapeDtypeStruct(held.shape, f32),
        ],
        in_specs=[in_vmem] * 3,
        out_specs=[in_vmem] * 2,
        input_output_aliases={0: 1},
        compiler_params=pltpu.CompilerParams(vmem_limit_bytes=grant),
    )(vmem(held), *pair)


def mix_kernel(mat, chunk, late, same, differ, *refs):
    sums, near, factors = refs[:edges], refs[edges : 2 * edges], refs[2 * edges :]
    mixed, next_rx, next_ry, held, new_rx, new_ry, sems, new_sems = refs[-8:]
    rank = sums[0].shape[0]
    width = edges * rank
    mats, rows, _ = held.shape
    steps = rows // chunk
    mine = steps - (late if mat < mats - 1 else 0)

    def copy(which, row, size, sem):
        here = pl.ds(row, size)
        return pltpu.make_async_copy(
            held.at[which, here], mixed.at[0, 0, which, here], sems.at[sem]
        )

    left = [copy(mat - 1, rows - late * chunk, late * chunk, steps)] if mat and late else []
    for other in left:
        other.start()
    if mat:
        factor = inverse_of(factors[0][:, -128:] + factors[1][:, -128:], rank)
    else:
        factor = factors[0][...]
    factor = factor[:, width : 2 * width]
    total = jnp.concatenate([b[...] + n[...] for b, n in zip(sums, near)], 0)
    updated = lax.dot_general(
        factor, total, NN, precision=lax.Precision.HIGHEST, preferred_element_type=f32
    )
    right = mixing * lax.dot_general(
        factor, updated, TN, precision=lax.Precision.HIGHEST, preferred_element_type=f32
    )
    r_high, r_low = split(right)
    terms = jnp.concatenate([r_high, r_high, r_low, r_low], 0)

    def correct(row, size):
        here = pl.ds(row, size)
        high, low = split(differ[:, here])
        lhs = jnp.concatenate([high, low, high, low], 0)
        held[mat, here, :] -= dot(lhs, terms, TN)

    halves = [copy(mat, 0, chunk // 2, 0), copy(mat, chunk // 2, chunk // 2, steps + 1)]
    for half in range(2):
        correct(half * (chunk // 2), chunk // 2)
        halves[half].start()

    def place(step):
        return pl.multiple_of(step * chunk, chunk)

    @pl.loop(1, mine)
    def _(step):
        correct(place(step), chunk)
        copy(mat, place(step), chunk, step).start()

    @pl.loop(mine, steps)
    def _(step):
        correct(place(step), chunk)

    parts = [updated[slot * rank : (slot + 1) * rank] for slot in range(edges)]
    new_rx[...] = jnp.where(odd("rx"), parts[2], parts[3])
    new_ry[...] = jnp.where(odd("ry"), parts[0], parts[1])
    new_copies = [
        pltpu.make_async_copy(new_rx, next_rx.at[0, 0, mat], new_sems.at[0]),
        pltpu.make_async_copy(new_ry, next_ry.at[0, 0, mat], new_sems.at[1]),
    ]
    for new_copy in new_copies:
        new_copy.start()
    for half in halves:
        half.wait()

    @pl.loop(1, mine)
    def _(step):
        copy(mat, place(step), chunk, step).wait()

    for other in left + new_copies:
        other.wait()


def mix(held, differ, factors, sums, near, mat, shapes, previous):
    mats, rows, features = held.shape
    rank = sums[0].shape[0]
    chunk = chunk_of(rows, 512)
    steps = rows // chunk
    args = [vmem(held), differ, *sums, *near, *factors]
    specs = [in_vmem] * len(args) + [in_hbm] * len(previous)
    aliases = {0: 3} | {len(args) + place: place for place in range(len(previous))}
    args += [hbm(array) for array in previous]
    shapes = (*shapes, held.shape)
    return pl.pallas_call(
        functools.partial(mix_kernel, mat, chunk, 3 * steps // 8),
        name=f"mix{mat}",
        out_shape=[jax.ShapeDtypeStruct(shape, f32) for shape in shapes],
        in_specs=specs,
        out_specs=[in_hbm] * 3 + [in_vmem],
        scratch_shapes=[
            pltpu.VMEM((rank, features), f32),
            pltpu.VMEM((rank, features), f32),
            pltpu.SemaphoreType.DMA((steps + 2,)),
            pltpu.SemaphoreType.DMA((2,)),
        ],
        input_output_aliases=aliases,
        cost_estimate=cost(held, 2),
        compiler_params=pltpu.CompilerParams(vmem_limit_bytes=grant),
    )(*args)


def per_device(weights, factors_rx, factors_ry):
    mats, rows = weights.shape[2:4]
    rank = factors_rx.shape[-2]
    lower_ry = shifted(factors_ry, "ry", 1)
    lower_rx = shifted(factors_rx, "rx", 1)
    factors = [factors_ry, lower_ry, factors_rx, lower_rx]
    size = chunk_of(rows, 512)
    pieces = rows // size
    ahead = max(pieces // 2, 1)
    until = ahead
    held = load(weights, size, until)
    own = []
    for mat in range(mats):
        first, until = until, min((mat + 1) * pieces + ahead, mats * pieces)
        *own_mat, held = project(held, factors, weights, mat, size, first, until)
        own.append(own_mat)
    near = [exchange(own_mat) for own_mat in own]
    differs, pairs = [], []
    tp = lax.axis_size("tp")
    for mat in range(mats):
        p, terms, held = back(held, own[mat], near[mat], mat)
        distance = 1
        while 2 * distance < tp:
            terms = terms + from_partner(terms, "tp", distance)
            distance *= 2
        other = from_partner(terms, "tp", distance) if tp > 1 else jnp.zeros_like(terms)
        differs.append(p)
        pairs.append((terms, other))
    sums, near_sums = [], []
    for mat in range(mats):
        *sum_mat, held = add(held, pairs[mat], rank, mat)
        sums.append(sum_mat)
        near_sums.append(exchange(sum_mat))
        if mat == 0:
            inverse, held = inverse_factor(held, pairs[0], rank)
    results = []
    shapes = (weights.shape, factors_rx.shape, factors_ry.shape)
    for mat in range(mats):
        factor = pairs[mat] if mat else [inverse]
        *results, held = mix(
            held, differs[mat], factor, sums[mat], near_sums[mat], mat, shapes, results
        )
    return tuple(results)


def solution(mesh):
    return jax.shard_map(
        per_device,
        mesh=mesh,
        in_specs=(
            P("rx", "ry", None, "tp", None),
            P("rx", "ry", None, None, None),
            P("rx", "ry", None, None, None),
        ),
        out_specs=(
            P("rx", "ry", None, "tp", None),
            P("rx", "ry", None, None, None),
            P("rx", "ry", None, None, None),
        ),
        check_vma=False,
    )
```

```python
import functools

import jax
import jax.numpy as jnp
from jax import lax
from jax.experimental import pallas as pl
from jax.experimental.pallas import tpu as pltpu
from jax.sharding import PartitionSpec as P

f32 = jnp.float32
bf16 = jnp.bfloat16
mixing = 0.2
edges = 4
grant = 8 << 20

NN = (((1,), (0,)), ((), ()))
NT = (((1,), (1,)), ((), ()))
TN = (((0,), (0,)), ((), ()))

in_vmem = pl.BlockSpec(memory_space=pltpu.VMEM)
in_hbm = pl.BlockSpec(memory_space=pltpu.HBM)


def vmem(value):
    return pltpu.with_memory_space_constraint(value, pltpu.VMEM)


def hbm(value):
    return pltpu.with_memory_space_constraint(value, pltpu.HBM)


def cost(held, passes):
    _, rows, features = held.shape
    flops = passes * 2 * 256 * rows * features
    return pl.CostEstimate(flops=flops, bytes_accessed=8 * rows * features, transcendentals=0)


def dot(a, b, dims):
    return lax.dot_general(a, b, dims, preferred_element_type=f32)


def split(value):
    high = value.astype(bf16)
    return high, (value - high.astype(f32)).astype(bf16)


def chunk_of(rows, most):
    size = min(rows, most)
    while rows % size:
        size //= 2
    return size


def chunks_of(rows, size):
    if rows % (4 * size):
        return [(0, rows)]
    return [(0, rows // 2), (rows // 2, rows // 4), (3 * rows // 4, rows // 4)]


def shifted(value, axis, steps):
    count = lax.axis_size(axis)
    pairs = [(source, (source + steps) % count) for source in range(count)]
    return lax.ppermute(value, axis, pairs)


def from_partner(value, axis, distance):
    count = lax.axis_size(axis)
    return lax.ppermute(value, axis, [(i, i ^ distance) for i in range(count)])


def exchange(values):
    swapped = []
    for slot, value in enumerate(values):
        axis, colour = ("ry", "rx")[slot // 2], 1 - slot % 2
        count = lax.axis_size(axis)
        pairs = [(i, (i + (1 if i % 2 == colour else -1)) % count) for i in range(count)]
        swapped.append(lax.ppermute(value, axis, pairs))
    return swapped


def odd(axis):
    return lax.rem(lax.axis_index(axis), 2) == 1


def piece_copy(weights, held, sems, size, mat, row, sem):
    here = pl.ds(row, size)
    return pltpu.make_async_copy(weights.at[0, 0, mat, here], held.at[mat, here], sems.at[sem])


def piece_copies(weights, held, sems, size, first, until):
    rows = held.shape[1]
    places = [divmod(piece * size, rows) for piece in range(first, until)]
    return [
        piece_copy(weights, held, sems, size, mat, row, sem)
        for sem, (mat, row) in enumerate(places)
    ]


def load_kernel(size, until, weights, held, sems):
    copies = piece_copies(weights, held, sems, size, 0, until)
    for copy in copies:
        copy.start()
    for copy in copies:
        copy.wait()


def load(weights, size, until):
    return pl.pallas_call(
        functools.partial(load_kernel, size, until),
        name="load",
        out_shape=jax.ShapeDtypeStruct(weights.shape[2:], f32),
        in_specs=[in_hbm],
        out_specs=in_vmem,
        scratch_shapes=[pltpu.SemaphoreType.DMA((until,))],
        compiler_params=pltpu.CompilerParams(vmem_limit_bytes=grant),
    )(hbm(weights))


def project_kernel(phase, extra, size, first, until, same, f0, f1, f2, f3, weights, *refs):
    *outs, held, sems = refs
    mats, rows, _ = held.shape
    pieces = rows // size
    copies = piece_copies(weights, held, sems, size, first, until)
    for copy in copies:
        copy.start()
    rank = f0.shape[-2]
    width = edges * rank

    def stack_of(mat):
        slots = []
        for axis, own, lower in (("ry", f0, f1), ("rx", f2, f3)):
            own, lower, swap = own[0, 0, mat], lower[0, 0, mat], odd(axis)
            slots += [jnp.where(swap, own, lower), jnp.where(swap, lower, own)]
        high, low = split(jnp.concatenate(slots, 0))
        return jnp.concatenate(
            [jnp.concatenate([high, high], 1), jnp.concatenate([low, low], 1)], 0
        )

    def step(mat, stack, row, chunk, place):
        for part in range(chunk // size):
            piece = row // size + part

            @pl.when(mat * pieces + piece >= first)
            def _():
                start = pl.multiple_of(piece * size, size)
                sem = mat * pieces + piece - first
                piece_copy(weights, held, sems, size, mat, start, sem).wait()

        w_high, w_low = split(held[mat, pl.ds(row, chunk), :])
        both = dot(stack, jnp.concatenate([w_high, w_low], 1), NT)
        total = both[:width] + both[width:]
        for slot, out in enumerate(outs):
            out[:, pl.ds(place, chunk)] = total[slot * rank : (slot + 1) * rank]

    skip = extra if phase else 0
    stack = stack_of(phase)
    chunk = chunk_of(rows, 1024)
    lead = chunk - skip if skip else 0
    if lead:
        step(phase, stack, skip, lead, 0)

    @pl.loop(1 if lead else 0, rows // chunk)
    def _(index):
        row = pl.multiple_of(index * chunk, chunk)
        step(phase, stack, row, chunk, pl.multiple_of(row - skip, min(chunk, extra or chunk)))

    taken = (phase + 1) * pieces
    if extra and phase < mats - 1:
        step(phase + 1, stack_of(phase + 1), 0, extra, rows - skip)
        taken += extra // size
    for copy in copies[taken - first :]:
        copy.wait()


def project(held, factors, weights, phase, extra, size, first, until):
    mats, rows, _ = held.shape
    rank = factors[0].shape[-2]
    columns = rows - (extra if phase else 0) + (extra if phase < mats - 1 else 0)
    return pl.pallas_call(
        functools.partial(project_kernel, phase, extra, size, first, until),
        name=f"project{phase}",
        out_shape=[jax.ShapeDtypeStruct((rank, columns), f32)] * edges
        + [jax.ShapeDtypeStruct(held.shape, f32)],
        in_specs=[in_vmem] * 5 + [in_hbm],
        out_specs=[in_vmem] * (edges + 1),
        scratch_shapes=[pltpu.SemaphoreType.DMA((max(until - first, 1),))],
        input_output_aliases={0: edges},
        cost_estimate=cost(held, 2),
        compiler_params=pltpu.CompilerParams(vmem_limit_bytes=grant),
    )(vmem(held), *factors, hbm(weights))


def back_kernel(mat, extra, same, *refs):
    *refs, differ, sums, held = refs
    ends = list(zip(refs[: len(refs) // 2], refs[len(refs) // 2 :]))
    rank = ends[0][0].shape[0]
    width = edges * rank
    _, rows, features = held.shape
    last = ends[-edges:]
    parts = []
    if len(ends) > edges:
        begin = ends[0][0].shape[1] - extra
        parts.append([o[:, begin:] - n[:, begin:] for o, n in ends[:edges]])
    rest = rows - (extra if parts else 0)
    parts.append([o[:, :rest] - n[:, :rest] for o, n in last])
    p = jnp.concatenate([jnp.concatenate(part, 0) for part in parts], 1)
    differ[...] = p
    high, low = split(p)
    w_high, w_low = split(held[mat])
    pair = jnp.concatenate([high, low], 0)
    stack = jnp.concatenate([pair, pair], 1)
    both = dot(stack, jnp.concatenate([w_high, w_low], 0), NN)
    sums[...] = jnp.zeros_like(sums)
    sums[:, :features] = both[:width] + both[width:]
    gram = dot(pair, pair, NT)
    total = (gram[:width, :width] + gram[width:, width:]) + (
        gram[:width, width:] + gram[width:, :width]
    )
    for edge in range(edges):
        here = slice(edge * rank, (edge + 1) * rank)
        sums[here, features : features + rank] = total[here, here]


def back(held, own, near, mat, extra):
    _, rows, features = held.shape
    rank = own[mat][0].shape[0]
    phases = [mat - 1, mat] if mat and extra else [mat]
    ends = [value for phase in phases for value in own[phase]]
    ends += [value for phase in phases for value in near[phase]]
    return pl.pallas_call(
        functools.partial(back_kernel, mat, extra),
        name=f"back{mat}",
        out_shape=[
            jax.ShapeDtypeStruct((edges * rank, rows), f32),
            jax.ShapeDtypeStruct((edges * rank, features + 128), f32),
            jax.ShapeDtypeStruct(held.shape, f32),
        ],
        in_specs=[in_vmem] * (1 + len(ends)),
        out_specs=[in_vmem] * 3,
        input_output_aliases={0: 2},
        cost_estimate=cost(held, 2),
        compiler_params=pltpu.CompilerParams(vmem_limit_bytes=grant),
    )(vmem(held), *ends)


def add_kernel(same, mine, other, *refs):
    *outs, held = refs
    rank, features = outs[0].shape
    for slot, out in enumerate(outs):
        here = slice(slot * rank, (slot + 1) * rank)
        out[...] = mine[here, :features] + other[here, :features]


def add(held, pair, rank, mat):
    sums = jax.ShapeDtypeStruct((rank, held.shape[-1]), f32)
    return pl.pallas_call(
        add_kernel,
        name=f"add{mat}",
        out_shape=[sums] * edges + [jax.ShapeDtypeStruct(held.shape, f32)],
        in_specs=[in_vmem] * 3,
        out_specs=[in_vmem] * (edges + 1),
        input_output_aliases={0: edges},
        compiler_params=pltpu.CompilerParams(vmem_limit_bytes=grant),
    )(vmem(held), *pair)


def inverse_of(gram, rank):
    width = edges * rank
    shape = (edges, rank, 128)
    row = lax.broadcasted_iota(jnp.int32, shape, 1)
    lane = lax.broadcasted_iota(jnp.int32, shape, 2)
    slot = lax.broadcasted_iota(jnp.int32, shape, 0)
    value = gram.reshape(shape)
    value = jnp.where(lane < rank, value, (lane == width + slot * rank + row).astype(f32))
    pivots = jnp.ones((edges, rank, 1), f32)
    for j in range(rank):
        pivot = value[:, j : j + 1, j : j + 1]
        pivots = jnp.where(row[:, :, :1] == j, pivot, pivots)
        factor = jnp.where(row > j, value[:, :, j : j + 1] / pivot, 0.0)
        value = value - factor * value[:, j : j + 1, :]
    return (value / jnp.sqrt(pivots)).reshape(width, 128)


def inverse_kernel(rank, same, mine, other, inverse, held):
    inverse[...] = inverse_of(mine[:, -128:] + other[:, -128:], rank)


def inverse_factor(held, pair, rank):
    return pl.pallas_call(
        functools.partial(inverse_kernel, rank),
        name="inverse",
        out_shape=[
            jax.ShapeDtypeStruct((edges * rank, 128), f32),
            jax.ShapeDtypeStruct(held.shape, f32),
        ],
        in_specs=[in_vmem] * 3,
        out_specs=[in_vmem] * 2,
        input_output_aliases={0: 1},
        compiler_params=pltpu.CompilerParams(vmem_limit_bytes=grant),
    )(vmem(held), *pair)


def mix_kernel(mat, chunk, late, same, differ, *refs):
    sums, near, factors = refs[:edges], refs[edges : 2 * edges], refs[2 * edges :]
    mixed, next_rx, next_ry, held, new_rx, new_ry, sems, new_sems = refs[-8:]
    rank = sums[0].shape[0]
    width = edges * rank
    mats, rows, _ = held.shape
    steps = rows // chunk
    mine = steps - (late if mat < mats - 1 else 0)

    def copy(which, row, size, sem):
        here = pl.ds(row, size)
        return pltpu.make_async_copy(
            held.at[which, here], mixed.at[0, 0, which, here], sems.at[sem]
        )

    left = [copy(mat - 1, rows - late * chunk, late * chunk, steps)] if mat and late else []
    for other in left:
        other.start()
    if mat:
        factor = inverse_of(factors[0][:, -128:] + factors[1][:, -128:], rank)
    else:
        factor = factors[0][...]
    factor = factor[:, width : 2 * width]
    total = jnp.concatenate([b[...] + n[...] for b, n in zip(sums, near)], 0)
    updated = lax.dot_general(
        factor, total, NN, precision=lax.Precision.HIGHEST, preferred_element_type=f32
    )
    right = mixing * lax.dot_general(
        factor, updated, TN, precision=lax.Precision.HIGHEST, preferred_element_type=f32
    )
    r_high, r_low = split(right)
    terms = jnp.concatenate([r_high, r_high, r_low, r_low], 0)

    def correct(row, size):
        here = pl.ds(row, size)
        high, low = split(differ[:, here])
        lhs = jnp.concatenate([high, low, high, low], 0)
        held[mat, here, :] -= dot(lhs, terms, TN)

    halves = [copy(mat, 0, chunk // 2, 0), copy(mat, chunk // 2, chunk // 2, steps + 1)]
    for half in range(2):
        correct(half * (chunk // 2), chunk // 2)
        halves[half].start()

    def place(step):
        return pl.multiple_of(step * chunk, chunk)

    @pl.loop(1, mine)
    def _(step):
        correct(place(step), chunk)
        copy(mat, place(step), chunk, step).start()

    @pl.loop(mine, steps)
    def _(step):
        correct(place(step), chunk)

    parts = [updated[slot * rank : (slot + 1) * rank] for slot in range(edges)]
    new_rx[...] = jnp.where(odd("rx"), parts[2], parts[3])
    new_ry[...] = jnp.where(odd("ry"), parts[0], parts[1])
    new_copies = [
        pltpu.make_async_copy(new_rx, next_rx.at[0, 0, mat], new_sems.at[0]),
        pltpu.make_async_copy(new_ry, next_ry.at[0, 0, mat], new_sems.at[1]),
    ]
    for new_copy in new_copies:
        new_copy.start()
    for half in halves:
        half.wait()

    @pl.loop(1, mine)
    def _(step):
        copy(mat, place(step), chunk, step).wait()

    for other in left + new_copies:
        other.wait()


def mix(held, differ, factors, sums, near, mat, shapes, previous):
    mats, rows, features = held.shape
    rank = sums[0].shape[0]
    chunk = chunk_of(rows, 512)
    steps = rows // chunk
    args = [vmem(held), differ, *sums, *near, *factors]
    specs = [in_vmem] * len(args) + [in_hbm] * len(previous)
    aliases = {0: 3} | {len(args) + place: place for place in range(len(previous))}
    args += [hbm(array) for array in previous]
    shapes = (*shapes, held.shape)
    return pl.pallas_call(
        functools.partial(mix_kernel, mat, chunk, 3 * steps // 8),
        name=f"mix{mat}",
        out_shape=[jax.ShapeDtypeStruct(shape, f32) for shape in shapes],
        in_specs=specs,
        out_specs=[in_hbm] * 3 + [in_vmem],
        scratch_shapes=[
            pltpu.VMEM((rank, features), f32),
            pltpu.VMEM((rank, features), f32),
            pltpu.SemaphoreType.DMA((steps + 2,)),
            pltpu.SemaphoreType.DMA((2,)),
        ],
        input_output_aliases=aliases,
        cost_estimate=cost(held, 2),
        compiler_params=pltpu.CompilerParams(vmem_limit_bytes=grant),
    )(*args)


def per_device(weights, factors_rx, factors_ry):
    mats, rows = weights.shape[2:4]
    rank = factors_rx.shape[-2]
    lower_ry = shifted(factors_ry, "ry", 1)
    lower_rx = shifted(factors_rx, "rx", 1)
    factors = [factors_ry, lower_ry, factors_rx, lower_rx]
    size = chunk_of(rows, 512)
    pieces = rows // size
    ahead = max(pieces // 2, 1)
    extra = size if pieces % 8 == 0 else 0
    until = ahead
    held = load(weights, size, until)
    own = []
    for mat in range(mats):
        first, until = until, min((mat + 1) * pieces + ahead, mats * pieces)
        *own_mat, held = project(held, factors, weights, mat, extra, size, first, until)
        own.append(own_mat)
    near = [exchange(own_mat) for own_mat in own]
    differs, pairs = [], []
    tp = lax.axis_size("tp")
    for mat in range(mats):
        p, terms, held = back(held, own, near, mat, extra)
        distance = 1
        while 2 * distance < tp:
            terms = terms + from_partner(terms, "tp", distance)
            distance *= 2
        other = from_partner(terms, "tp", distance) if tp > 1 else jnp.zeros_like(terms)
        differs.append(p)
        pairs.append((terms, other))
    sums, near_sums = [], []
    for mat in range(mats):
        *sum_mat, held = add(held, pairs[mat], rank, mat)
        sums.append(sum_mat)
        near_sums.append(exchange(sum_mat))
        if mat == 0:
            inverse, held = inverse_factor(held, pairs[0], rank)
    results = []
    shapes = (weights.shape, factors_rx.shape, factors_ry.shape)
    for mat in range(mats):
        factor = pairs[mat] if mat else [inverse]
        *results, held = mix(
            held, differs[mat], factor, sums[mat], near_sums[mat], mat, shapes, results
        )
    return tuple(results)


def solution(mesh):
    return jax.shard_map(
        per_device,
        mesh=mesh,
        in_specs=(
            P("rx", "ry", None, "tp", None),
            P("rx", "ry", None, None, None),
            P("rx", "ry", None, None, None),
        ),
        out_specs=(
            P("rx", "ry", None, "tp", None),
            P("rx", "ry", None, None, None),
            P("rx", "ry", None, None, None),
        ),
        check_vma=False,
    )
```

```python
import functools

import jax
import jax.numpy as jnp
from jax import lax
from jax.experimental import pallas as pl
from jax.experimental.pallas import tpu as pltpu
from jax.sharding import PartitionSpec as P

f32 = jnp.float32
bf16 = jnp.bfloat16
mixing = 0.2
edges = 4
grant = 8 << 20

NN = (((1,), (0,)), ((), ()))
NT = (((1,), (1,)), ((), ()))
TN = (((0,), (0,)), ((), ()))

in_vmem = pl.BlockSpec(memory_space=pltpu.VMEM)
in_hbm = pl.BlockSpec(memory_space=pltpu.HBM)


def vmem(value):
    return pltpu.with_memory_space_constraint(value, pltpu.VMEM)


def hbm(value):
    return pltpu.with_memory_space_constraint(value, pltpu.HBM)


def cost(held, passes):
    _, rows, features = held.shape
    flops = passes * 2 * 256 * rows * features
    return pl.CostEstimate(flops=flops, bytes_accessed=8 * rows * features, transcendentals=0)


def dot(a, b, dims):
    return lax.dot_general(a, b, dims, preferred_element_type=f32)


def split(value):
    high = value.astype(bf16)
    return high, (value - high.astype(f32)).astype(bf16)


def chunk_of(rows, most):
    size = min(rows, most)
    while rows % size:
        size //= 2
    return size


def chunks_of(rows, size):
    if rows % (4 * size):
        return [(0, rows)]
    return [(0, rows // 2), (rows // 2, rows // 4), (3 * rows // 4, rows // 4)]


def shifted(value, axis, steps):
    count = lax.axis_size(axis)
    pairs = [(source, (source + steps) % count) for source in range(count)]
    return lax.ppermute(value, axis, pairs)


def from_partner(value, axis, distance):
    count = lax.axis_size(axis)
    return lax.ppermute(value, axis, [(i, i ^ distance) for i in range(count)])


def exchange(values):
    swapped = []
    for slot, value in enumerate(values):
        axis, colour = ("ry", "rx")[slot // 2], 1 - slot % 2
        count = lax.axis_size(axis)
        pairs = [(i, (i + (1 if i % 2 == colour else -1)) % count) for i in range(count)]
        swapped.append(lax.ppermute(value, axis, pairs))
    return swapped


def odd(axis):
    return lax.rem(lax.axis_index(axis), 2) == 1


def piece_copy(weights, held, sems, size, mat, row, sem):
    here = pl.ds(row, size)
    return pltpu.make_async_copy(weights.at[0, 0, mat, here], held.at[mat, here], sems.at[sem])


def piece_copies(weights, held, sems, size, first, until):
    rows = held.shape[1]
    places = [divmod(piece * size, rows) for piece in range(first, until)]
    return [
        piece_copy(weights, held, sems, size, mat, row, sem)
        for sem, (mat, row) in enumerate(places)
    ]


def load_kernel(size, until, weights, held, sems):
    copies = piece_copies(weights, held, sems, size, 0, until)
    for copy in copies:
        copy.start()
    for copy in copies:
        copy.wait()


def load(weights, size, until):
    return pl.pallas_call(
        functools.partial(load_kernel, size, until),
        name="load",
        out_shape=jax.ShapeDtypeStruct(weights.shape[2:], f32),
        in_specs=[in_hbm],
        out_specs=in_vmem,
        scratch_shapes=[pltpu.SemaphoreType.DMA((until,))],
        compiler_params=pltpu.CompilerParams(vmem_limit_bytes=grant),
    )(hbm(weights))


def project_kernel(phase, extra, size, first, until, same, f0, f1, f2, f3, weights, *refs):
    *outs, held, sems = refs
    mats, rows, _ = held.shape
    pieces = rows // size
    copies = piece_copies(weights, held, sems, size, first, until)
    for copy in copies:
        copy.start()
    rank = f0.shape[-2]
    width = edges * rank

    def stack_of(mat):
        slots = []
        for axis, own, lower in (("ry", f0, f1), ("rx", f2, f3)):
            own, lower, swap = own[0, 0, mat], lower[0, 0, mat], odd(axis)
            slots += [jnp.where(swap, own, lower), jnp.where(swap, lower, own)]
        high, low = split(jnp.concatenate(slots, 0))
        return jnp.concatenate(
            [jnp.concatenate([high, high], 1), jnp.concatenate([low, low], 1)], 0
        )

    def step(mat, stack, row, chunk, place):
        for part in range(chunk // size):
            piece = row // size + part

            @pl.when(mat * pieces + piece >= first)
            def _():
                start = pl.multiple_of(piece * size, size)
                sem = mat * pieces + piece - first
                piece_copy(weights, held, sems, size, mat, start, sem).wait()

        w_high, w_low = split(held[mat, pl.ds(row, chunk), :])
        both = dot(stack, jnp.concatenate([w_high, w_low], 1), NT)
        total = both[:width] + both[width:]
        for slot, out in enumerate(outs):
            out[:, pl.ds(place, chunk)] = total[slot * rank : (slot + 1) * rank]

    skip = extra if phase else 0
    stack = stack_of(phase)
    chunk = chunk_of(rows, 1024)
    lead = chunk - skip if skip else min(2 * chunk, rows)
    step(phase, stack, skip, lead, 0)

    @pl.loop((skip + lead) // chunk, rows // chunk)
    def _(index):
        row = pl.multiple_of(index * chunk, chunk)
        step(phase, stack, row, chunk, pl.multiple_of(row - skip, min(chunk, extra or chunk)))

    taken = (phase + 1) * pieces
    if extra and phase < mats - 1:
        step(phase + 1, stack_of(phase + 1), 0, extra, rows - skip)
        taken += extra // size
    for copy in copies[taken - first :]:
        copy.wait()


def project(held, factors, weights, phase, extra, size, first, until):
    mats, rows, _ = held.shape
    rank = factors[0].shape[-2]
    columns = rows - (extra if phase else 0) + (extra if phase < mats - 1 else 0)
    return pl.pallas_call(
        functools.partial(project_kernel, phase, extra, size, first, until),
        name=f"project{phase}",
        out_shape=[jax.ShapeDtypeStruct((rank, columns), f32)] * edges
        + [jax.ShapeDtypeStruct(held.shape, f32)],
        in_specs=[in_vmem] * 5 + [in_hbm],
        out_specs=[in_vmem] * (edges + 1),
        scratch_shapes=[pltpu.SemaphoreType.DMA((max(until - first, 1),))],
        input_output_aliases={0: edges},
        cost_estimate=cost(held, 2),
        compiler_params=pltpu.CompilerParams(vmem_limit_bytes=grant),
    )(vmem(held), *factors, hbm(weights))


def back_kernel(mat, extra, same, *refs):
    *refs, differ, sums, held = refs
    ends = list(zip(refs[: len(refs) // 2], refs[len(refs) // 2 :]))
    rank = ends[0][0].shape[0]
    width = edges * rank
    _, rows, features = held.shape
    last = ends[-edges:]
    parts = []
    if len(ends) > edges:
        begin = ends[0][0].shape[1] - extra
        parts.append([o[:, begin:] - n[:, begin:] for o, n in ends[:edges]])
    rest = rows - (extra if parts else 0)
    parts.append([o[:, :rest] - n[:, :rest] for o, n in last])
    p = jnp.concatenate([jnp.concatenate(part, 0) for part in parts], 1)
    differ[...] = p
    high, low = split(p)
    w_high, w_low = split(held[mat])
    pair = jnp.concatenate([high, low], 0)
    stack = jnp.concatenate([pair, pair], 1)
    both = dot(stack, jnp.concatenate([w_high, w_low], 0), NN)
    sums[...] = jnp.zeros_like(sums)
    sums[:, :features] = both[:width] + both[width:]
    gram = dot(pair, pair, NT)
    total = (gram[:width, :width] + gram[width:, width:]) + (
        gram[:width, width:] + gram[width:, :width]
    )
    for edge in range(edges):
        here = slice(edge * rank, (edge + 1) * rank)
        sums[here, features : features + rank] = total[here, here]


def back(held, own, near, mat, extra):
    _, rows, features = held.shape
    rank = own[mat][0].shape[0]
    phases = [mat - 1, mat] if mat and extra else [mat]
    ends = [value for phase in phases for value in own[phase]]
    ends += [value for phase in phases for value in near[phase]]
    return pl.pallas_call(
        functools.partial(back_kernel, mat, extra),
        name=f"back{mat}",
        out_shape=[
            jax.ShapeDtypeStruct((edges * rank, rows), f32),
            jax.ShapeDtypeStruct((edges * rank, features + 128), f32),
            jax.ShapeDtypeStruct(held.shape, f32),
        ],
        in_specs=[in_vmem] * (1 + len(ends)),
        out_specs=[in_vmem] * 3,
        input_output_aliases={0: 2},
        cost_estimate=cost(held, 2),
        compiler_params=pltpu.CompilerParams(vmem_limit_bytes=grant),
    )(vmem(held), *ends)


def add_kernel(same, mine, other, *refs):
    *outs, held = refs
    rank, features = outs[0].shape
    for slot, out in enumerate(outs):
        here = slice(slot * rank, (slot + 1) * rank)
        out[...] = mine[here, :features] + other[here, :features]


def add(held, pair, rank, mat):
    sums = jax.ShapeDtypeStruct((rank, held.shape[-1]), f32)
    return pl.pallas_call(
        add_kernel,
        name=f"add{mat}",
        out_shape=[sums] * edges + [jax.ShapeDtypeStruct(held.shape, f32)],
        in_specs=[in_vmem] * 3,
        out_specs=[in_vmem] * (edges + 1),
        input_output_aliases={0: edges},
        compiler_params=pltpu.CompilerParams(vmem_limit_bytes=grant),
    )(vmem(held), *pair)


def inverse_of(gram, rank):
    width = edges * rank
    shape = (edges, rank, 128)
    row = lax.broadcasted_iota(jnp.int32, shape, 1)
    lane = lax.broadcasted_iota(jnp.int32, shape, 2)
    slot = lax.broadcasted_iota(jnp.int32, shape, 0)
    value = gram.reshape(shape)
    value = jnp.where(lane < rank, value, (lane == width + slot * rank + row).astype(f32))
    pivots = jnp.ones((edges, rank, 1), f32)
    for j in range(rank):
        pivot = value[:, j : j + 1, j : j + 1]
        pivots = jnp.where(row[:, :, :1] == j, pivot, pivots)
        factor = jnp.where(row > j, value[:, :, j : j + 1] / pivot, 0.0)
        value = value - factor * value[:, j : j + 1, :]
    return (value / jnp.sqrt(pivots)).reshape(width, 128)


def inverse_kernel(rank, same, mine, other, inverse, held):
    inverse[...] = inverse_of(mine[:, -128:] + other[:, -128:], rank)


def inverse_factor(held, pair, rank):
    return pl.pallas_call(
        functools.partial(inverse_kernel, rank),
        name="inverse",
        out_shape=[
            jax.ShapeDtypeStruct((edges * rank, 128), f32),
            jax.ShapeDtypeStruct(held.shape, f32),
        ],
        in_specs=[in_vmem] * 3,
        out_specs=[in_vmem] * 2,
        input_output_aliases={0: 1},
        compiler_params=pltpu.CompilerParams(vmem_limit_bytes=grant),
    )(vmem(held), *pair)


def mix_kernel(mat, chunk, late, same, differ, *refs):
    sums, near, factors = refs[:edges], refs[edges : 2 * edges], refs[2 * edges :]
    mixed, next_rx, next_ry, held, new_rx, new_ry, sems, new_sems = refs[-8:]
    rank = sums[0].shape[0]
    width = edges * rank
    mats, rows, _ = held.shape
    steps = rows // chunk
    mine = steps - (late if mat < mats - 1 else 0)

    def copy(which, row, size, sem):
        here = pl.ds(row, size)
        return pltpu.make_async_copy(
            held.at[which, here], mixed.at[0, 0, which, here], sems.at[sem]
        )

    left = [copy(mat - 1, rows - late * chunk, late * chunk, steps)] if mat and late else []
    for other in left:
        other.start()
    if mat:
        factor = inverse_of(factors[0][:, -128:] + factors[1][:, -128:], rank)
    else:
        factor = factors[0][...]
    factor = factor[:, width : 2 * width]
    total = jnp.concatenate([b[...] + n[...] for b, n in zip(sums, near)], 0)
    updated = lax.dot_general(
        factor, total, NN, precision=lax.Precision.HIGHEST, preferred_element_type=f32
    )
    right = mixing * lax.dot_general(
        factor, updated, TN, precision=lax.Precision.HIGHEST, preferred_element_type=f32
    )
    r_high, r_low = split(right)
    terms = jnp.concatenate([r_high, r_high, r_low, r_low], 0)

    def correct(row, size):
        here = pl.ds(row, size)
        high, low = split(differ[:, here])
        lhs = jnp.concatenate([high, low, high, low], 0)
        held[mat, here, :] -= dot(lhs, terms, TN)

    halves = [copy(mat, 0, chunk // 2, 0), copy(mat, chunk // 2, chunk // 2, steps + 1)]
    for half in range(2):
        correct(half * (chunk // 2), chunk // 2)
        halves[half].start()

    def place(step):
        return pl.multiple_of(step * chunk, chunk)

    @pl.loop(1, mine)
    def _(step):
        correct(place(step), chunk)
        copy(mat, place(step), chunk, step).start()

    @pl.loop(mine, steps)
    def _(step):
        correct(place(step), chunk)

    parts = [updated[slot * rank : (slot + 1) * rank] for slot in range(edges)]
    new_rx[...] = jnp.where(odd("rx"), parts[2], parts[3])
    new_ry[...] = jnp.where(odd("ry"), parts[0], parts[1])
    new_copies = [
        pltpu.make_async_copy(new_rx, next_rx.at[0, 0, mat], new_sems.at[0]),
        pltpu.make_async_copy(new_ry, next_ry.at[0, 0, mat], new_sems.at[1]),
    ]
    for new_copy in new_copies:
        new_copy.start()
    for half in halves:
        half.wait()

    @pl.loop(1, mine)
    def _(step):
        copy(mat, place(step), chunk, step).wait()

    for other in left + new_copies:
        other.wait()


def mix(held, differ, factors, sums, near, mat, shapes, previous):
    mats, rows, features = held.shape
    rank = sums[0].shape[0]
    chunk = chunk_of(rows, 512)
    steps = rows // chunk
    args = [vmem(held), differ, *sums, *near, *factors]
    specs = [in_vmem] * len(args) + [in_hbm] * len(previous)
    aliases = {0: 3} | {len(args) + place: place for place in range(len(previous))}
    args += [hbm(array) for array in previous]
    shapes = (*shapes, held.shape)
    return pl.pallas_call(
        functools.partial(mix_kernel, mat, chunk, 3 * steps // 8),
        name=f"mix{mat}",
        out_shape=[jax.ShapeDtypeStruct(shape, f32) for shape in shapes],
        in_specs=specs,
        out_specs=[in_hbm] * 3 + [in_vmem],
        scratch_shapes=[
            pltpu.VMEM((rank, features), f32),
            pltpu.VMEM((rank, features), f32),
            pltpu.SemaphoreType.DMA((steps + 2,)),
            pltpu.SemaphoreType.DMA((2,)),
        ],
        input_output_aliases=aliases,
        cost_estimate=cost(held, 2),
        compiler_params=pltpu.CompilerParams(vmem_limit_bytes=grant),
    )(*args)


def per_device(weights, factors_rx, factors_ry):
    mats, rows = weights.shape[2:4]
    rank = factors_rx.shape[-2]
    lower_ry = shifted(factors_ry, "ry", 1)
    lower_rx = shifted(factors_rx, "rx", 1)
    factors = [factors_ry, lower_ry, factors_rx, lower_rx]
    size = chunk_of(rows, 512)
    pieces = rows // size
    ahead = max(pieces // 2, 1)
    extra = size if pieces % 8 == 0 else 0
    until = ahead
    held = load(weights, size, until)
    own = []
    for mat in range(mats):
        first, until = until, min((mat + 1) * pieces + ahead, mats * pieces)
        *own_mat, held = project(held, factors, weights, mat, extra, size, first, until)
        own.append(own_mat)
    near = [exchange(own_mat) for own_mat in own]
    differs, pairs = [], []
    tp = lax.axis_size("tp")
    for mat in range(mats):
        p, terms, held = back(held, own, near, mat, extra)
        distance = 1
        while 2 * distance < tp:
            terms = terms + from_partner(terms, "tp", distance)
            distance *= 2
        other = from_partner(terms, "tp", distance) if tp > 1 else jnp.zeros_like(terms)
        differs.append(p)
        pairs.append((terms, other))
    sums, near_sums = [], []
    for mat in range(mats):
        *sum_mat, held = add(held, pairs[mat], rank, mat)
        sums.append(sum_mat)
        near_sums.append(exchange(sum_mat))
        if mat == 0:
            inverse, held = inverse_factor(held, pairs[0], rank)
    results = []
    shapes = (weights.shape, factors_rx.shape, factors_ry.shape)
    for mat in range(mats):
        factor = pairs[mat] if mat else [inverse]
        *results, held = mix(
            held, differs[mat], factor, sums[mat], near_sums[mat], mat, shapes, results
        )
    return tuple(results)


def solution(mesh):
    return jax.shard_map(
        per_device,
        mesh=mesh,
        in_specs=(
            P("rx", "ry", None, "tp", None),
            P("rx", "ry", None, None, None),
            P("rx", "ry", None, None, None),
        ),
        out_specs=(
            P("rx", "ry", None, "tp", None),
            P("rx", "ry", None, None, None),
            P("rx", "ry", None, None, None),
        ),
        check_vma=False,
    )
```

```python
import functools

import jax
import jax.numpy as jnp
from jax import lax
from jax.experimental import pallas as pl
from jax.experimental.pallas import tpu as pltpu
from jax.sharding import PartitionSpec as P

f32 = jnp.float32
bf16 = jnp.bfloat16
mixing = 0.2
edges = 4
grant = 8 << 20

NN = (((1,), (0,)), ((), ()))
NT = (((1,), (1,)), ((), ()))
TN = (((0,), (0,)), ((), ()))

in_vmem = pl.BlockSpec(memory_space=pltpu.VMEM)
in_hbm = pl.BlockSpec(memory_space=pltpu.HBM)


def vmem(value):
    return pltpu.with_memory_space_constraint(value, pltpu.VMEM)


def hbm(value):
    return pltpu.with_memory_space_constraint(value, pltpu.HBM)


def cost(held, passes):
    _, rows, features = held.shape
    flops = passes * 2 * 256 * rows * features
    return pl.CostEstimate(flops=flops, bytes_accessed=8 * rows * features, transcendentals=0)


def dot(a, b, dims):
    return lax.dot_general(a, b, dims, preferred_element_type=f32)


def split(value):
    high = value.astype(bf16)
    return high, (value - high.astype(f32)).astype(bf16)


def chunk_of(rows, most):
    size = min(rows, most)
    while rows % size:
        size //= 2
    return size


def chunks_of(rows, size):
    if rows % (4 * size):
        return [(0, rows)]
    return [(0, rows // 2), (rows // 2, rows // 4), (3 * rows // 4, rows // 4)]


def shifted(value, axis, steps):
    count = lax.axis_size(axis)
    pairs = [(source, (source + steps) % count) for source in range(count)]
    return lax.ppermute(value, axis, pairs)


def from_partner(value, axis, distance):
    count = lax.axis_size(axis)
    return lax.ppermute(value, axis, [(i, i ^ distance) for i in range(count)])


def exchange(values):
    swapped = []
    for slot, value in enumerate(values):
        axis, colour = ("ry", "rx")[slot // 2], 1 - slot % 2
        count = lax.axis_size(axis)
        pairs = [(i, (i + (1 if i % 2 == colour else -1)) % count) for i in range(count)]
        swapped.append(lax.ppermute(value, axis, pairs))
    return swapped


def odd(axis):
    return lax.rem(lax.axis_index(axis), 2) == 1


def piece_copy(weights, held, sems, size, mat, row, sem):
    here = pl.ds(row, size)
    return pltpu.make_async_copy(weights.at[0, 0, mat, here], held.at[mat, here], sems.at[sem])


def piece_copies(weights, held, sems, size, first, until):
    rows = held.shape[1]
    places = [divmod(piece * size, rows) for piece in range(first, until)]
    return [
        piece_copy(weights, held, sems, size, mat, row, sem)
        for sem, (mat, row) in enumerate(places)
    ]


def load_kernel(size, until, weights, held, sems):
    copies = piece_copies(weights, held, sems, size, 0, until)
    for copy in copies:
        copy.start()
    for copy in copies:
        copy.wait()


def load(weights, size, until):
    return pl.pallas_call(
        functools.partial(load_kernel, size, until),
        name="load",
        out_shape=jax.ShapeDtypeStruct(weights.shape[2:], f32),
        in_specs=[in_hbm],
        out_specs=in_vmem,
        scratch_shapes=[pltpu.SemaphoreType.DMA((until,))],
        compiler_params=pltpu.CompilerParams(vmem_limit_bytes=grant),
    )(hbm(weights))


def project_kernel(phase, extra, size, first, until, same, f0, f1, f2, f3, weights, *refs):
    *outs, held, sems = refs
    mats, rows, _ = held.shape
    pieces = rows // size
    copies = piece_copies(weights, held, sems, size, first, until)
    for copy in copies:
        copy.start()
    rank = f0.shape[-2]
    width = edges * rank

    def stack_of(mat):
        slots = []
        for axis, own, lower in (("ry", f0, f1), ("rx", f2, f3)):
            own, lower, swap = own[0, 0, mat], lower[0, 0, mat], odd(axis)
            slots += [jnp.where(swap, own, lower), jnp.where(swap, lower, own)]
        high, low = split(jnp.concatenate(slots, 0))
        return jnp.concatenate(
            [jnp.concatenate([high, high], 1), jnp.concatenate([low, low], 1)], 0
        )

    def step(mat, stack, row, chunk, place):
        for part in range(chunk // size):
            piece = row // size + part

            @pl.when(mat * pieces + piece >= first)
            def _():
                start = pl.multiple_of(piece * size, size)
                sem = mat * pieces + piece - first
                piece_copy(weights, held, sems, size, mat, start, sem).wait()

        w_high, w_low = split(held[mat, pl.ds(row, chunk), :])
        both = dot(stack, jnp.concatenate([w_high, w_low], 1), NT)
        total = both[:width] + both[width:]
        for slot, out in enumerate(outs):
            out[:, pl.ds(place, chunk)] = total[slot * rank : (slot + 1) * rank]

    skip = extra if phase else 0
    stack = stack_of(phase)
    chunk = chunk_of(rows, 1024)
    lead = chunk - skip if skip else 0
    if lead:
        step(phase, stack, skip, lead, 0)

    @pl.loop(1 if lead else 0, rows // chunk)
    def _(index):
        row = pl.multiple_of(index * chunk, chunk)
        step(phase, stack, row, chunk, pl.multiple_of(row - skip, min(chunk, extra or chunk)))

    taken = (phase + 1) * pieces
    if extra and phase < mats - 1:
        step(phase + 1, stack_of(phase + 1), 0, extra, rows - skip)
        taken += extra // size
    for copy in copies[taken - first :]:
        copy.wait()


def project(held, factors, weights, phase, extra, size, first, until):
    mats, rows, _ = held.shape
    rank = factors[0].shape[-2]
    columns = rows - (extra if phase else 0) + (extra if phase < mats - 1 else 0)
    return pl.pallas_call(
        functools.partial(project_kernel, phase, extra, size, first, until),
        name=f"project{phase}",
        out_shape=[jax.ShapeDtypeStruct((rank, columns), f32)] * edges
        + [jax.ShapeDtypeStruct(held.shape, f32)],
        in_specs=[in_vmem] * 5 + [in_hbm],
        out_specs=[in_vmem] * (edges + 1),
        scratch_shapes=[pltpu.SemaphoreType.DMA((max(until - first, 1),))],
        input_output_aliases={0: edges},
        cost_estimate=cost(held, 2),
        compiler_params=pltpu.CompilerParams(vmem_limit_bytes=grant),
    )(vmem(held), *factors, hbm(weights))


def back_kernel(mat, extra, same, *refs):
    *refs, differ, sums, held = refs
    ends = list(zip(refs[: len(refs) // 2], refs[len(refs) // 2 :]))
    rank = ends[0][0].shape[0]
    width = edges * rank
    _, rows, features = held.shape
    last = ends[-edges:]
    parts = []
    if len(ends) > edges:
        begin = ends[0][0].shape[1] - extra
        parts.append([o[:, begin:] - n[:, begin:] for o, n in ends[:edges]])
    rest = rows - (extra if parts else 0)
    parts.append([o[:, :rest] - n[:, :rest] for o, n in last])
    p = jnp.concatenate([jnp.concatenate(part, 0) for part in parts], 1)
    differ[...] = p
    high, low = split(p)
    w_high, w_low = split(held[mat])
    pair = jnp.concatenate([high, low], 0)
    stack = jnp.concatenate([pair, pair], 1)
    both = dot(stack, jnp.concatenate([w_high, w_low], 0), NN)
    product = both[:width] + both[width:]
    for block in range(features // 128):
        sums[block * width : (block + 1) * width] = product[:, block * 128 : (block + 1) * 128]
    sums[features // 128 * width :] = jnp.zeros((rank, 128), f32)
    gram = dot(pair, pair, NT)
    total = (gram[:width, :width] + gram[width:, width:]) + (
        gram[:width, width:] + gram[width:, :width]
    )
    for edge in range(edges):
        here = slice(edge * rank, (edge + 1) * rank)
        sums[features // 128 * width :, here] = total[here, here]


def back(held, own, near, mat, extra):
    _, rows, features = held.shape
    rank = own[mat][0].shape[0]
    phases = [mat - 1, mat] if mat and extra else [mat]
    ends = [value for phase in phases for value in own[phase]]
    ends += [value for phase in phases for value in near[phase]]
    return pl.pallas_call(
        functools.partial(back_kernel, mat, extra),
        name=f"back{mat}",
        out_shape=[
            jax.ShapeDtypeStruct((edges * rank, rows), f32),
            jax.ShapeDtypeStruct((features // 128 * edges * rank + rank, 128), f32),
            jax.ShapeDtypeStruct(held.shape, f32),
        ],
        in_specs=[in_vmem] * (1 + len(ends)),
        out_specs=[in_vmem] * 3,
        input_output_aliases={0: 2},
        cost_estimate=cost(held, 2),
        compiler_params=pltpu.CompilerParams(vmem_limit_bytes=grant),
    )(vmem(held), *ends)


def add_kernel(same, mine, other, *refs):
    *outs, held = refs
    rank, features = outs[0].shape
    for slot, out in enumerate(outs):
        for block in range(features // 128):
            start = block * edges * rank + slot * rank
            here = slice(start, start + rank)
            out[:, block * 128 : (block + 1) * 128] = mine[here] + other[here]


def add(held, pair, rank, mat):
    sums = jax.ShapeDtypeStruct((rank, held.shape[-1]), f32)
    return pl.pallas_call(
        add_kernel,
        name=f"add{mat}",
        out_shape=[sums] * edges + [jax.ShapeDtypeStruct(held.shape, f32)],
        in_specs=[in_vmem] * 3,
        out_specs=[in_vmem] * (edges + 1),
        input_output_aliases={0: edges},
        compiler_params=pltpu.CompilerParams(vmem_limit_bytes=grant),
    )(vmem(held), *pair)


def inverse_of(gram, rank):
    width = edges * rank
    shape = (edges, rank, 128)
    row = lax.broadcasted_iota(jnp.int32, shape, 1)
    lane = lax.broadcasted_iota(jnp.int32, shape, 2)
    slot = lax.broadcasted_iota(jnp.int32, shape, 0)
    turned = [gram] + [pltpu.roll(gram, 128 - edge * rank, 1) for edge in range(1, edges)]
    value = jnp.concatenate(turned, 0).reshape(shape)
    value = jnp.where(lane < rank, value, (lane == width + slot * rank + row).astype(f32))
    pivots = jnp.ones((edges, rank, 1), f32)
    for j in range(rank):
        pivot = value[:, j : j + 1, j : j + 1]
        pivots = jnp.where(row[:, :, :1] == j, pivot, pivots)
        factor = jnp.where(row > j, value[:, :, j : j + 1] / pivot, 0.0)
        value = value - factor * value[:, j : j + 1, :]
    return (value / jnp.sqrt(pivots)).reshape(width, 128)[:, width : 2 * width]


def inverse_kernel(rank, same, mine, other, inverse, held):
    inverse[...] = inverse_of(mine[-rank:, :] + other[-rank:, :], rank)


def inverse_factor(held, pair, rank):
    return pl.pallas_call(
        functools.partial(inverse_kernel, rank),
        name="inverse",
        out_shape=[
            jax.ShapeDtypeStruct((edges * rank, edges * rank), f32),
            jax.ShapeDtypeStruct(held.shape, f32),
        ],
        in_specs=[in_vmem] * 3,
        out_specs=[in_vmem] * 2,
        input_output_aliases={0: 1},
        compiler_params=pltpu.CompilerParams(vmem_limit_bytes=grant),
    )(vmem(held), *pair)


def mix_kernel(mat, chunk, late, same, differ, *refs):
    sums, near, factors = refs[:edges], refs[edges : 2 * edges], refs[2 * edges :]
    mixed, next_rx, next_ry, held, new_rx, new_ry, sems, new_sems = refs[-8:]
    rank = sums[0].shape[0]
    width = edges * rank
    mats, rows, _ = held.shape
    steps = rows // chunk
    mine = steps - (late if mat < mats - 1 else 0)

    def copy(which, row, size, sem):
        here = pl.ds(row, size)
        return pltpu.make_async_copy(
            held.at[which, here], mixed.at[0, 0, which, here], sems.at[sem]
        )

    left = [copy(mat - 1, rows - late * chunk, late * chunk, steps)] if mat and late else []
    for other in left:
        other.start()
    if mat:
        factor = inverse_of(factors[0][-rank:, :] + factors[1][-rank:, :], rank)
    else:
        factor = factors[0][...]
    total = jnp.concatenate([b[...] + n[...] for b, n in zip(sums, near)], 0)
    updated = lax.dot_general(
        factor, total, NN, precision=lax.Precision.HIGHEST, preferred_element_type=f32
    )
    right = mixing * lax.dot_general(
        factor, updated, TN, precision=lax.Precision.HIGHEST, preferred_element_type=f32
    )
    r_high, r_low = split(right)
    terms = jnp.concatenate([r_high, r_high, r_low, r_low], 0)

    def correct(row, size):
        here = pl.ds(row, size)
        high, low = split(differ[:, here])
        lhs = jnp.concatenate([high, low, high, low], 0)
        held[mat, here, :] -= dot(lhs, terms, TN)

    cut = chunk // 2
    halves = [copy(mat, 0, cut, 0), copy(mat, cut, chunk - cut, steps + 1)]
    correct(0, cut)
    halves[0].start()
    correct(cut, chunk - cut)
    halves[1].start()

    def place(step):
        return pl.multiple_of(step * chunk, chunk)

    @pl.loop(1, mine)
    def _(step):
        correct(place(step), chunk)
        copy(mat, place(step), chunk, step).start()

    @pl.loop(mine, steps)
    def _(step):
        correct(place(step), chunk)

    parts = [updated[slot * rank : (slot + 1) * rank] for slot in range(edges)]
    new_rx[...] = jnp.where(odd("rx"), parts[2], parts[3])
    new_ry[...] = jnp.where(odd("ry"), parts[0], parts[1])
    new_copies = [
        pltpu.make_async_copy(new_rx, next_rx.at[0, 0, mat], new_sems.at[0]),
        pltpu.make_async_copy(new_ry, next_ry.at[0, 0, mat], new_sems.at[1]),
    ]
    for new_copy in new_copies:
        new_copy.start()
    for half in halves:
        half.wait()

    @pl.loop(1, mine)
    def _(step):
        copy(mat, place(step), chunk, step).wait()

    for other in left + new_copies:
        other.wait()


def mix(held, differ, factors, sums, near, mat, shapes, previous):
    mats, rows, features = held.shape
    rank = sums[0].shape[0]
    chunk = chunk_of(rows, 512)
    steps = rows // chunk
    args = [vmem(held), differ, *sums, *near, *factors]
    specs = [in_vmem] * len(args) + [in_hbm] * len(previous)
    aliases = {0: 3} | {len(args) + place: place for place in range(len(previous))}
    args += [hbm(array) for array in previous]
    shapes = (*shapes, held.shape)
    return pl.pallas_call(
        functools.partial(mix_kernel, mat, chunk, steps // 4),
        name=f"mix{mat}",
        out_shape=[jax.ShapeDtypeStruct(shape, f32) for shape in shapes],
        in_specs=specs,
        out_specs=[in_hbm] * 3 + [in_vmem],
        scratch_shapes=[
            pltpu.VMEM((rank, features), f32),
            pltpu.VMEM((rank, features), f32),
            pltpu.SemaphoreType.DMA((steps + 2,)),
            pltpu.SemaphoreType.DMA((2,)),
        ],
        input_output_aliases=aliases,
        cost_estimate=cost(held, 2),
        compiler_params=pltpu.CompilerParams(vmem_limit_bytes=grant),
    )(*args)


def per_device(weights, factors_rx, factors_ry):
    mats, rows = weights.shape[2:4]
    rank = factors_rx.shape[-2]
    lower_ry = shifted(factors_ry, "ry", 1)
    lower_rx = shifted(factors_rx, "rx", 1)
    factors = [factors_ry, lower_ry, factors_rx, lower_rx]
    size = chunk_of(rows, 512)
    pieces = rows // size
    ahead = max(pieces // 2, 1)
    extra = size if pieces % 8 == 0 else 0
    until = ahead
    held = load(weights, size, until)
    own = []
    for mat in range(mats):
        first, until = until, min((mat + 1) * pieces + ahead, mats * pieces)
        *own_mat, held = project(held, factors, weights, mat, extra, size, first, until)
        own.append(own_mat)
    near = [exchange(own_mat) for own_mat in own]
    differs, pairs = [], []
    tp = lax.axis_size("tp")
    for mat in range(mats):
        p, terms, held = back(held, own, near, mat, extra)
        distance = 1
        while 2 * distance < tp:
            terms = terms + from_partner(terms, "tp", distance)
            distance *= 2
        other = from_partner(terms, "tp", distance) if tp > 1 else jnp.zeros_like(terms)
        differs.append(p)
        pairs.append((terms, other))
    sums, near_sums = [], []
    for mat in range(mats):
        *sum_mat, held = add(held, pairs[mat], rank, mat)
        sums.append(sum_mat)
        near_sums.append(exchange(sum_mat))
        if mat == 0:
            inverse, held = inverse_factor(held, pairs[0], rank)
    results = []
    shapes = (weights.shape, factors_rx.shape, factors_ry.shape)
    for mat in range(mats):
        factor = pairs[mat] if mat else [inverse]
        *results, held = mix(
            held, differs[mat], factor, sums[mat], near_sums[mat], mat, shapes, results
        )
    return tuple(results)


def solution(mesh):
    return jax.shard_map(
        per_device,
        mesh=mesh,
        in_specs=(
            P("rx", "ry", None, "tp", None),
            P("rx", "ry", None, None, None),
            P("rx", "ry", None, None, None),
        ),
        out_specs=(
            P("rx", "ry", None, "tp", None),
            P("rx", "ry", None, None, None),
            P("rx", "ry", None, None, None),
        ),
        check_vma=False,
    )
```
